32 devices in a mesh: blk: 8 (over z, core), grp: 4 (over y, x).
Axes of the slice: x: 2, y: 2, z: 4, core: 2. Of those that a mesh axis runs over, the one named last changes fastest.
Arguments:
- signal: bfloat16 [4, 64, 4096], P('grp', None, 'blk'), may hold values from -10 to 10
- lag_table: int32 [512], replicated, may hold values from 0 to 511, each once
- window_end: int32 [4, 8], P('grp', 'blk'), may hold values from 128 to 512
Outputs:
- factors: float32 [4, 512, 512], P('grp', 'blk')
- coeffs: float32 [4, 512, 64], P('grp', 'blk')
- residual: float32 [4, 64, 4096], P('grp', None, 'blk')
The draws below stay inside these ranges and needn't reach their ends.
Inputs may be any that keep to these rules, and one draw needn't show every extreme that they name: `lag_table`: each of 0 to 511 appears once.
All inputs are finite; a program needn't handle non-finite values.
Results may differ from the reference program's by a relative error of at most 0.0003.
Values may be sent and summed in bfloat16 or wider, within the bound.
A program may use at most 192 MiB of HBM per device.

```python
import math
import jax
import jax.numpy as jnp
from jax import lax

SENSORS = 64
LAGS = 8
ROWS = 512
COLS = 512
NBLOCKS = 8
NGROUPS = 4
SPAN = 4096


period_steps = 64


def draw_signal(key, part):
    key_list = jax.random.split(key, 5)
    group_times = jnp.arange(NGROUPS, dtype=jnp.int32)[:, None] * SPAN + jnp.arange(SPAN, dtype=jnp.int32)[None, :]
    frequency = jax.random.randint(key_list[0], (SENSORS,), 1, period_steps // 2)
    turn_index = group_times[:, None, :] * frequency[None, :, None] % period_steps
    phases = jax.random.uniform(key_list[1], (SENSORS,), jnp.float32, -math.pi, math.pi)
    wave_part = 0.7 * jnp.sin(2.0 * math.pi * turn_index.astype(jnp.float32) / period_steps + phases[None, :, None])
    levels = jax.random.uniform(key_list[2], (NGROUPS, 1, NBLOCKS, 1), jnp.float32, 0.5, 1.5)
    noise_part = jnp.clip(jax.random.normal(key_list[3], (NGROUPS, SENSORS, NBLOCKS, ROWS), jnp.float32), -4.0, 4.0)
    scales = jax.random.uniform(key_list[4], (SENSORS,), jnp.float32, 0.7, 1.4)
    rough_part = (noise_part * levels).reshape(NGROUPS, SENSORS, SPAN)
    values = scales[None, :, None] * (wave_part + rough_part)
    return values.astype(jnp.bfloat16)


def draw_window_end(key, part):
    key_list = jax.random.split(key, 2)
    ends_flat = jax.random.randint(key_list[0], (NGROUPS * NBLOCKS,), ROWS // 4, ROWS + 1)
    positions = jax.random.permutation(key_list[1], NGROUPS * NBLOCKS)
    ends_flat = ends_flat.at[positions[0]].set(ROWS).at[positions[1]].set(ROWS // 4)
    return ends_flat.reshape(NGROUPS, NBLOCKS).astype(jnp.int32)


def setup_inputs(seed: int = 0) -> dict:
    splits = jax.random.split(jax.random.key(seed), 4)
    return {
        "signal": draw_signal(jax.random.fold_in(splits[3], 71), 0),
        "lag_table": jax.random.permutation(splits[1], COLS).astype(jnp.int32),
        "window_end": draw_window_end(jax.random.fold_in(splits[3], 71), 0),
    }


ridge_weight = 4.0

def lagged_block(history, row_start, block_len, lag_count):
    pieces = [lax.dynamic_slice_in_dim(history, row_start + (lag_count - 1 - delay_index), block_len, 1) for delay_index in range(lag_count)]
    return jnp.concatenate(pieces, axis=0)

def highest(first_matrix, second_matrix):
    return jnp.dot(first_matrix, second_matrix, precision=lax.Precision.HIGHEST)

def reference(signal, lag_table, window_end):
    block_len = min(512, ROWS)
    per_group = SPAN // block_len
    series = jnp.transpose(signal, (1, 0, 2)).reshape(SENSORS, NGROUPS * SPAN)
    padded = jnp.concatenate([jnp.zeros((SENSORS, LAGS), signal.dtype), series], axis=1)

    def group_history(group_index):
        return lax.dynamic_slice_in_dim(padded, (group_index * SPAN).astype(jnp.int32), SPAN + LAGS, 1)

    def group_terms(group_index):
        history = group_history(group_index)
        group_ends = window_end[group_index]

        def add_block(carry_pair, step_index):
            gram_part, cross_part = carry_pair
            row_start = (step_index * block_len).astype(jnp.int32)
            lagged = lagged_block(history, row_start, block_len, LAGS).astype(jnp.float32)
            target = lax.dynamic_slice_in_dim(history, row_start + LAGS, block_len, 1).astype(jnp.float32)
            device = row_start // ROWS
            local_rows = row_start % ROWS + jnp.arange(block_len, dtype=jnp.int32)
            live_mask = local_rows < group_ends[device]
            masked = jnp.where(live_mask[None, :], lagged, jnp.zeros_like(lagged))
            gram_part = gram_part + jnp.dot(masked.astype(jnp.float32), lagged.T.astype(jnp.float32), preferred_element_type=jnp.float32)
            cross_part = cross_part + jnp.dot(masked.astype(jnp.float32), target.T.astype(jnp.float32), preferred_element_type=jnp.float32)
            return ((gram_part, cross_part), None)
        start_gram = NBLOCKS * ridge_weight * jnp.eye(COLS, dtype=jnp.float32)
        start_cross = jnp.zeros((COLS, SENSORS), jnp.float32)
        sums_pair, unused = lax.scan(add_block, (start_gram, start_cross), jnp.arange(per_group, dtype=jnp.int32))
        return sums_pair
    grams, crosses = lax.map(group_terms, jnp.arange(NGROUPS, dtype=jnp.int32))
    prefix_grams = jnp.cumsum(grams, axis=0)
    prefix_crosses = jnp.cumsum(crosses, axis=0)

    def solve_group(sums_pair):
        gram_part, cross_part = sums_pair
        ordered = gram_part[lag_table][:, lag_table]
        lower_factor = jnp.linalg.cholesky(ordered)
        half_solved = lax.linalg.triangular_solve(lower_factor, cross_part[lag_table], left_side=True, lower=True)
        coefficients = lax.linalg.triangular_solve(lower_factor, half_solved, left_side=True, lower=True, transpose_a=True)
        return (lower_factor.T / math.sqrt(SPAN), coefficients)
    factors, coeffs = lax.map(solve_group, (prefix_grams, prefix_crosses))

    def group_residual(group_index):
        history = group_history(group_index)
        canonical = jnp.zeros((COLS, SENSORS), coeffs.dtype).at[lag_table].set(coeffs[group_index])

        def one_block(step_index):
            row_start = (step_index * block_len).astype(jnp.int32)
            lagged = lagged_block(history, row_start, block_len, LAGS).astype(jnp.float32)
            target = lax.dynamic_slice_in_dim(history, row_start + LAGS, block_len, 1).astype(jnp.float32)
            return target - highest(canonical.T, lagged)
        pieces = lax.map(one_block, jnp.arange(per_group, dtype=jnp.int32))
        return jnp.transpose(pieces, (1, 0, 2)).reshape(SENSORS, SPAN)
    residual = lax.map(group_residual, jnp.arange(NGROUPS, dtype=jnp.int32))
    return (factors, coeffs, residual)
```

```python
import functools
import math

import jax
import jax.numpy as jnp
from jax import lax
from jax.experimental import pallas as pl
from jax.experimental.pallas import tpu as pltpu
from jax.sharding import PartitionSpec as P

ridge_weight = 4.0
LAGS = 8
TILE = 128
WIDE = 640
MESH = pl.DeviceIdType.MESH
VMEM = pltpu.VMEM
F32 = jnp.float32
BF16 = jnp.bfloat16


def iota(shape, dim):
    return lax.broadcasted_iota(jnp.int32, shape, dim)


def dot(a, b):
    return jnp.dot(a, b, preferred_element_type=F32)


def dot_nt(a, b):
    return lax.dot_general(a, b, (((1,), (1,)), ((), ())), preferred_element_type=F32)


def exact_dot(a, b):
    return jnp.dot(a, b, precision=lax.Precision.HIGHEST, preferred_element_type=F32)


def split3(x):
    hi = x.astype(BF16)
    rest = x - hi.astype(F32)
    mid = rest.astype(BF16)
    low = (rest - mid.astype(F32)).astype(BF16)
    return hi, mid, low


def delayed(x, delay):
    if delay == 0:
        return x
    return jnp.where(iota(x.shape, 1) < delay, 0.0, pltpu.roll(x, delay, 1))


def moments_kernel(end_ref, x_ref, c_ref, e_ref):
    x = x_ref[0].astype(F32)
    sensors, rows = x.shape
    end = end_ref[0, 0]
    stack = [delayed(x, d) for d in range(LAGS + 1)] + [jnp.zeros_like(x)]
    z = jnp.concatenate(stack, axis=0).astype(BF16)
    xm = jnp.where(iota(x.shape, 1) < end, x, 0.0).astype(BF16)
    c_ref[...] = dot_nt(xm, z).reshape(c_ref.shape)
    row, time = iota((16, rows), 0), iota((16, rows), 1)
    head_tail = jnp.where(row < 8, row, rows - 16 + row)
    last_live = jnp.where(row < 8, -1, end - 16 + row)
    sel_a = jnp.where(time == head_tail, 1.0, 0.0).astype(BF16)
    sel_b = jnp.where(time == last_live, 1.0, 0.0).astype(BF16)
    xl = jnp.concatenate([x, jnp.zeros_like(x)], axis=0).astype(BF16)
    xr = jnp.concatenate([jnp.zeros_like(x), x], axis=0).astype(BF16)
    e_ref[...] = (dot_nt(sel_a, xl) + dot_nt(sel_b, xr)).astype(BF16)


def share_kernel(nblk, ngrp, ns, c_ref, e_ref, sum_ref, edge_ref,
                 part, group_edge, prior, all_edge, mine, whole,
                 send1, recv1, send1e, recv1e, send2, recv2, send2e, recv2e, send3, recv3):
    b, g = lax.axis_index("blk"), lax.axis_index("grp")
    owner = (lambda i: True) if ns == nblk else (lambda i: i < ns)

    def when(cond, fn):
        if cond is True:
            fn()
        else:
            pl.when(cond)(fn)

    prior[...] = jnp.zeros_like(prior)
    all_edge[...] = jnp.zeros_like(all_edge)
    barrier = pltpu.get_barrier_semaphore()
    for off in range(1, nblk):
        pl.semaphore_signal(barrier, inc=1, device_id=(lax.rem(b + off, nblk), g), device_id_type=MESH)
    for off in range(1, ngrp):
        pl.semaphore_signal(barrier, inc=1, device_id=(b, lax.rem(g + off, ngrp)), device_id_type=MESH)
    pl.semaphore_wait(barrier, nblk - 1 + ngrp - 1)

    def slice_copy(to, frm, off):
        return pltpu.make_async_remote_copy(
            src_ref=c_ref.at[to], dst_ref=part.at[frm], send_sem=send1.at[off], recv_sem=recv1.at[frm],
            device_id=(to, g), device_id_type=MESH)

    def edge_copy(to, frm, off):
        return pltpu.make_async_remote_copy(
            src_ref=e_ref, dst_ref=group_edge.at[frm], send_sem=send1e.at[off], recv_sem=recv1e.at[frm],
            device_id=(to, g), device_id_type=MESH)

    for off in range(1, nblk):
        to = lax.rem(b + off, nblk)
        when(owner(to), lambda: slice_copy(to, b, off).start())
        edge_copy(to, b, off).start()
    when(owner(b), lambda: part.__setitem__(b, c_ref[b]))
    group_edge[b] = e_ref[...]
    for off in range(1, nblk):
        frm = lax.rem(b + nblk - off, nblk)
        when(owner(b), lambda: slice_copy(b, frm, off).wait_recv())
        edge_copy(b, frm, off).wait_recv()

    def total():
        acc = part[0]
        for i in range(1, nblk):
            acc = acc + part[i]
        mine[...] = acc

    when(owner(b), total)
    all_edge[g] = group_edge[...]

    def sum_copy(to, frm):
        return pltpu.make_async_remote_copy(
            src_ref=mine, dst_ref=prior.at[frm], send_sem=send2.at[to], recv_sem=recv2.at[frm],
            device_id=(b, to), device_id_type=MESH)

    def edges_copy(to, frm):
        return pltpu.make_async_remote_copy(
            src_ref=group_edge, dst_ref=all_edge.at[frm], send_sem=send2e.at[to], recv_sem=recv2e.at[frm],
            device_id=(b, to), device_id_type=MESH)

    for h in range(1, ngrp):
        @pl.when(h > g)
        def _():
            when(owner(b), lambda: sum_copy(h, g).start())
            edges_copy(h, g).start()
    for h in range(ngrp - 1):
        @pl.when(h < g)
        def _():
            when(owner(b), lambda: sum_copy(g, h).wait_recv())

    def prefix():
        acc = mine[...]
        for h in range(ngrp - 1):
            acc = acc + prior[h]
        whole[b] = acc

    when(owner(b), prefix)

    def whole_copy(to, frm, off):
        return pltpu.make_async_remote_copy(
            src_ref=whole.at[frm], dst_ref=whole.at[frm], send_sem=send3.at[off], recv_sem=recv3.at[frm],
            device_id=(to, g), device_id_type=MESH)

    for off in range(1, nblk):
        when(owner(b), lambda: whole_copy(lax.rem(b + off, nblk), b, off).start())
    for h in range(ngrp - 1):
        @pl.when(h < g)
        def _():
            edges_copy(g, h).wait_recv()
    edge_ref[...] = all_edge[...]
    for off in range(1, nblk):
        frm = lax.rem(b + nblk - off, nblk)
        when(owner(frm), lambda: whole_copy(b, frm, off).wait_recv())
    sum_ref[...] = whole[...]
    for off in range(1, nblk):
        to = lax.rem(b + off, nblk)
        when(owner(to), lambda: slice_copy(to, b, off).wait_send())
        edge_copy(to, b, off).wait_send()
        when(owner(b), lambda: whole_copy(to, b, off).wait_send())
    for h in range(1, ngrp):
        @pl.when(h > g)
        def _():
            when(owner(b), lambda: sum_copy(h, g).wait_send())
            edges_copy(h, g).wait_send()


def lower_inverse(block, out_ref, r0):
    n = TILE // 8
    lane, sub = iota((8, TILE), 1), iota((8, TILE), 0)
    x = [block[8 * r : 8 * r + 8, :] for r in range(n)]

    def rep_lane(v, j):
        return jnp.broadcast_to(v[:, j : j + 1], (8, TILE))

    def rep_row(v, i):
        return jnp.broadcast_to(v[i : i + 1, :], (8, TILE))

    for q in range(n):
        first = 8 * q
        cols = [rep_lane(x[q], first + j) for j in range(8)]
        t = {(i, j): rep_row(cols[j], i) for j in range(8) for i in range(j, 8)}
        inside = (lane >= first) & (lane < first + 8)
        aug = jnp.where(inside, jnp.where(lane - first == sub, 1.0, 0.0), x[q])
        y = [rep_row(aug, i) for i in range(8)]
        inv, l, scaled = [], {}, []
        for j in range(8):
            p = t[j, j]
            inv.append(1.0 / p)
            scaled.append(y[j] * lax.rsqrt(p))
            for i in range(j + 1, 8):
                l[i, j] = t[i, j] * inv[j]
            for k in range(j + 1, 8):
                for i in range(k, 8):
                    t[i, k] = t[i, k] - l[i, j] * t[k, j]
            for i in range(j + 1, 8):
                y[i] = y[i] - l[i, j] * y[j]
        rows = scaled[0]
        for i in range(1, 8):
            rows = jnp.where(sub == i, scaled[i], rows)
        out_ref[pl.ds(pl.multiple_of(r0 + first, 8), 8), :] = jnp.where(lane < first + 8, rows, 0.0)
        if q == n - 1:
            break
        gs = [None] * 8
        for i in range(7, -1, -1):
            acc = y[i] * inv[i]
            for k in range(7, i, -1):
                acc = acc - l[k, i] * gs[k]
            gs[i] = acc
        for r in range(q + 1, n):
            new = jnp.where(inside, 0.0, x[r])
            for j in range(7, -1, -1):
                new = new - rep_lane(x[r], first + j) * gs[j]
            x[r] = new


def fit_kernel(nblk, ngrp, x_ref, lagc_ref, lagr_ref, c_ref, e_ref, fac_ref, coef_ref, res_ref,
               a, ps, pe, tl, vt, dm, miss, u, li, w):
    b, g = lax.axis_index("blk"), lax.axis_index("grp")
    cols = a.shape[0]
    x = x_ref[0].astype(F32)
    sensors, rows = x.shape
    half = nblk * 8

    ps[...] = jnp.zeros_like(ps)
    pe[...] = jnp.zeros_like(pe)
    tl[...] = jnp.zeros_like(tl)
    dm[...] = jnp.zeros_like(dm)
    miss[...] = jnp.zeros_like(miss)
    lane3 = iota((nblk, 16, TILE), 2)
    left = iota((nblk, 8, TILE), 2) < sensors

    def group_edges(h, carry):
        e = e_ref[h].astype(F32)
        turned = pltpu.roll(e.reshape(nblk * 16, TILE), sensors, 1).reshape(nblk, 16, TILE)
        lo = jnp.where(lane3 < sensors, e, turned)
        hi = jnp.where(lane3 < sensors, turned, e)
        ps[0, 0:8, :] = tl[...]
        if nblk > 1:
            ps[1:, 0:8, :] = lo[: nblk - 1, 8:16, :]
        tl[...] = lo[nblk - 1, 8:16, :]
        pe[:, 0:8, :] = hi[:, 8:16, :]
        head = lo[:, 0:8, :].reshape(half, TILE)
        for i in range(LAGS // 2):
            even, odd = 2 * i + 1, 2 * i + 2
            for ref, at in ((ps, 0), (pe, half)):
                part = jnp.where(left, ref[:, pl.ds(8 - even, 8), :], ref[:, pl.ds(8 - odd, 8), :])
                vt[at : at + half, i * TILE : (i + 1) * TILE] = part.reshape(half, TILE)
        v = vt[...]
        signed = jnp.where(iota(v.shape, 0) < half, v, -v)
        v16 = v.astype(BF16)
        dm[...] += dot(signed.T.astype(BF16), v16)
        miss[...] += dot(head.T.astype(BF16), v16[:half])
        return carry

    lax.fori_loop(0, g + 1, group_edges, 0)

    more = jnp.concatenate([miss[0:sensors, :], jnp.zeros((sensors, TILE), F32)], axis=1)
    c = c_ref[...].reshape(sensors, WIDE) + pltpu.roll(more, sensors, 1)
    cm = jnp.where(iota(c.shape, 1) < sensors, 0.5 * c, c)
    cr = pltpu.roll(cm, sensors, 1)
    a[...] = jnp.zeros_like(a)
    for i in range(LAGS):
        base = sensors * (i - i % 2)
        a[sensors * i : sensors * (i + 1), base:cols] = (cr if i % 2 else cm)[:, : cols - base]
    gu = a[:, :cols]
    ridge = (ridge_weight * nblk) * (g + 1).astype(F32)
    eye = jnp.where(iota((cols, cols), 0) == iota((cols, cols), 1), ridge, 0.0)
    gram = gu + gu.T + dm[...] + eye
    cross = jnp.concatenate([c, jnp.zeros_like(c)], axis=0).T[sensors : sensors + cols, :]
    both = jnp.concatenate([gram, cross], axis=1)
    pick = jnp.where(lagc_ref[...] == iota((cols, cols), 1), 1.0, 0.0).astype(BF16)
    pick_t = jnp.where(lagr_ref[...] == iota((cols, cols), 0), 1.0, 0.0).astype(BF16)
    hi, mid, low = split3(both)
    turned = dot(pick, hi) + dot(pick, mid) + dot(pick, low)
    a[:, cols:] = turned[:, cols:]
    hi, mid, low = split3(turned[:, :cols])
    a[:, :cols] = dot(hi, pick_t) + dot(mid, pick_t) + dot(low, pick_t)

    steps = cols // TILE

    def eliminate(k, carry):
        r0 = pl.multiple_of(k * TILE, TILE)
        lower_inverse(a[pl.ds(r0, TILE), pl.ds(r0, TILE)], li, r0)
        panel = exact_dot(li[pl.ds(r0, TILE), :], a[pl.ds(r0, TILE), :])
        panel = jnp.where(iota(panel.shape, 1) >= iota(panel.shape, 0) + r0, panel, 0.0)
        u[pl.ds(r0, TILE), :] = panel

        @pl.when(k < steps - 1)
        def _():
            a[...] -= exact_dot(panel[:, :cols].T, panel)

        return carry

    lax.fori_loop(0, steps, eliminate, 0)

    w[...] = jnp.zeros_like(w)
    for k in range(steps - 1, -1, -1):
        at = slice(k * TILE, (k + 1) * TILE)
        rhs = u[at, cols:]
        if k < steps - 1:
            rhs = rhs - exact_dot(u[at, (k + 1) * TILE : cols], w[(k + 1) * TILE :, :])
        w[at, :] = exact_dot(li[at, :].T, rhs)

    share = cols // nblk
    row0 = pl.multiple_of(b * share, share)
    fac_ref[0] = u[pl.ds(row0, share), :cols] * (1.0 / math.sqrt(rows * nblk))
    coef_ref[0] = w[pl.ds(row0, share), :][:, :sensors]

    hi, mid, low = split3(w[...])
    canon = (dot(pick_t, hi) + dot(pick_t, mid) + dot(pick_t, low)).T[:sensors, :]
    hi, mid, low = split3(canon)
    z = jnp.concatenate([delayed(x, d) for d in range(1, LAGS + 1)], axis=0).astype(BF16)
    fitted = dot(hi, z) + dot(mid, z) + dot(low, z)
    own = vt[pl.ds(pl.multiple_of(b * 8, 8), 8), :]
    own = jnp.concatenate([own, jnp.zeros((TILE - 8, cols), F32)], axis=0).astype(BF16)
    rim = dot_nt(hi, own) + dot_nt(mid, own) + dot_nt(low, own)
    res = x - fitted
    res_ref[0, :, :TILE] = res[:, :TILE] - rim
    res_ref[0, :, TILE:] = res[:, TILE:]


def on_device(nblk, ngrp, signal, lag_table, window_end):
    _, sensors, rows = signal.shape
    cols = lag_table.shape[0]
    ns = min(nblk, sensors // 8)
    per = sensors // ns
    vmem = pl.BlockSpec(memory_space=VMEM)
    smem = pl.BlockSpec(memory_space=pltpu.SMEM)
    dma = pltpu.SemaphoreType.DMA
    c, e = pl.pallas_call(
        moments_kernel,
        out_shape=(jax.ShapeDtypeStruct((ns, per, WIDE), F32), jax.ShapeDtypeStruct((16, TILE), BF16)),
        in_specs=[smem, vmem],
        out_specs=(vmem, vmem),
    )(window_end, signal)
    sums, edges = pl.pallas_call(
        functools.partial(share_kernel, nblk, ngrp, ns),
        out_shape=(jax.ShapeDtypeStruct((ns, per, WIDE), F32),
                   jax.ShapeDtypeStruct((ngrp, nblk, 16, TILE), BF16)),
        in_specs=[vmem, vmem],
        out_specs=(vmem, vmem),
        scratch_shapes=[
            VMEM((nblk, per, WIDE), F32), VMEM((nblk, 16, TILE), BF16),
            VMEM((ngrp, per, WIDE), F32), VMEM((ngrp, nblk, 16, TILE), BF16),
            VMEM((per, WIDE), F32), VMEM((ns, per, WIDE), F32),
            dma((nblk,)), dma((nblk,)), dma((nblk,)), dma((nblk,)),
            dma((ngrp,)), dma((ngrp,)), dma((ngrp,)), dma((ngrp,)),
            dma((nblk,)), dma((nblk,)),
        ],
        compiler_params=pltpu.CompilerParams(
            collective_id=0, has_side_effects=True, vmem_limit_bytes=32 * 1024 * 1024),
    )(c, e)
    half = nblk * 8
    share = cols // nblk
    return pl.pallas_call(
        functools.partial(fit_kernel, nblk, ngrp),
        out_shape=(jax.ShapeDtypeStruct((1, share, cols), F32),
                   jax.ShapeDtypeStruct((1, share, sensors), F32),
                   jax.ShapeDtypeStruct((1, sensors, rows), F32)),
        in_specs=[vmem] * 5,
        out_specs=(vmem, vmem, vmem),
        scratch_shapes=[
            VMEM((cols, WIDE), F32), VMEM((nblk, 16, TILE), F32), VMEM((nblk, 16, TILE), F32),
            VMEM((8, TILE), F32), VMEM((2 * half, cols), F32), VMEM((cols, cols), F32),
            VMEM((TILE, cols), F32), VMEM((cols, WIDE), F32), VMEM((cols, TILE), F32),
            VMEM((cols, TILE), F32),
        ],
        compiler_params=pltpu.CompilerParams(vmem_limit_bytes=48 * 1024 * 1024),
    )(signal, lag_table.reshape(cols, 1), lag_table.reshape(1, cols), sums, edges)


def solution(mesh):
    return jax.shard_map(
        functools.partial(on_device, mesh.shape["blk"], mesh.shape["grp"]),
        mesh=mesh,
        in_specs=(P("grp", None, "blk"), P(), P("grp", "blk")),
        out_specs=(P("grp", "blk", None), P("grp", "blk", None), P("grp", None, "blk")),
        check_vma=False,
    )
```

```python
import functools
import math

import jax
import jax.numpy as jnp
from jax import lax
from jax.experimental import pallas as pl
from jax.experimental.pallas import tpu as pltpu
from jax.sharding import PartitionSpec as P

ridge_weight = 4.0
LAGS = 8
TILE = 128
WIDE = 640
MESH = pl.DeviceIdType.MESH
VMEM = pltpu.VMEM
F32 = jnp.float32
BF16 = jnp.bfloat16


def iota(shape, dim):
    return lax.broadcasted_iota(jnp.int32, shape, dim)


def dot(a, b):
    return jnp.dot(a, b, preferred_element_type=F32)


def dot_nt(a, b):
    return lax.dot_general(a, b, (((1,), (1,)), ((), ())), preferred_element_type=F32)


def exact_dot(a, b):
    return jnp.dot(a, b, precision=lax.Precision.HIGHEST, preferred_element_type=F32)


def split3(x):
    hi = x.astype(BF16)
    rest = x - hi.astype(F32)
    mid = rest.astype(BF16)
    low = (rest - mid.astype(F32)).astype(BF16)
    return hi, mid, low


def delayed(x, delay):
    if delay == 0:
        return x
    return jnp.where(iota(x.shape, 1) < delay, 0.0, pltpu.roll(x, delay, 1))


def moments(x, end):
    sensors, rows = x.shape
    stack = [delayed(x, d) for d in range(LAGS + 1)] + [jnp.zeros_like(x)]
    z = jnp.concatenate(stack, axis=0).astype(BF16)
    xm = jnp.where(iota(x.shape, 1) < end, x, 0.0).astype(BF16)
    c = dot_nt(xm, z)
    row, time = iota((16, rows), 0), iota((16, rows), 1)
    head_tail = jnp.where(row < 8, row, rows - 16 + row)
    last_live = jnp.where(row < 8, -1, end - 16 + row)
    sel_a = jnp.where(time == head_tail, 1.0, 0.0).astype(BF16)
    sel_b = jnp.where(time == last_live, 1.0, 0.0).astype(BF16)
    xl = jnp.concatenate([x, jnp.zeros_like(x)], axis=0).astype(BF16)
    xr = jnp.concatenate([jnp.zeros_like(x), x], axis=0).astype(BF16)
    return c, (dot_nt(sel_a, xl) + dot_nt(sel_b, xr)).astype(BF16)


def share_kernel(nblk, ngrp, ns, end_ref, x_ref, lag_ref, sum_ref, edge_ref, x_out, lagc_ref, lagr_ref,
                 c_ref, e_ref, part, group_edge, prior, all_edge, mine, whole,
                 send1, recv1, send1e, recv1e, send2, recv2, send2e, recv2e, send3, recv3):
    b, g = lax.axis_index("blk"), lax.axis_index("grp")
    owner = (lambda i: True) if ns == nblk else (lambda i: i < ns)

    def when(cond, fn):
        if cond is True:
            fn()
        else:
            pl.when(cond)(fn)

    prior[...] = jnp.zeros_like(prior)
    all_edge[...] = jnp.zeros_like(all_edge)
    barrier = pltpu.get_barrier_semaphore()
    for off in range(1, nblk):
        pl.semaphore_signal(barrier, inc=1, device_id=(lax.rem(b + off, nblk), g), device_id_type=MESH)
    for off in range(1, ngrp):
        pl.semaphore_signal(barrier, inc=1, device_id=(b, lax.rem(g + off, ngrp)), device_id_type=MESH)
    c, e = moments(x_ref[0].astype(F32), end_ref[0, 0])
    c_ref[...] = c.reshape(c_ref.shape)
    e_ref[...] = e
    pl.semaphore_wait(barrier, nblk - 1 + ngrp - 1)

    def slice_copy(to, frm, off):
        return pltpu.make_async_remote_copy(
            src_ref=c_ref.at[to], dst_ref=part.at[frm], send_sem=send1.at[off], recv_sem=recv1.at[frm],
            device_id=(to, g), device_id_type=MESH)

    def edge_copy(to, frm, off):
        return pltpu.make_async_remote_copy(
            src_ref=e_ref, dst_ref=group_edge.at[frm], send_sem=send1e.at[off], recv_sem=recv1e.at[frm],
            device_id=(to, g), device_id_type=MESH)

    for off in range(1, nblk):
        to = lax.rem(b + off, nblk)
        when(owner(to), lambda: slice_copy(to, b, off).start())
        edge_copy(to, b, off).start()
    when(owner(b), lambda: part.__setitem__(b, c_ref[b]))
    group_edge[b] = e_ref[...]
    x_out[...] = x_ref[0]
    lag = lag_ref[...].astype(F32)
    lagr_ref[...] = jnp.broadcast_to(lag, lagr_ref.shape)
    lagc_ref[...] = jnp.broadcast_to(lag, (TILE, lag.shape[1])).T
    for off in range(1, nblk):
        frm = lax.rem(b + nblk - off, nblk)
        when(owner(b), lambda: slice_copy(b, frm, off).wait_recv())
        edge_copy(b, frm, off).wait_recv()

    def total():
        acc = part[0]
        for i in range(1, nblk):
            acc = acc + part[i]
        mine[...] = acc

    when(owner(b), total)
    all_edge[g] = group_edge[...]

    def sum_copy(to, frm):
        return pltpu.make_async_remote_copy(
            src_ref=mine, dst_ref=prior.at[frm], send_sem=send2.at[to], recv_sem=recv2.at[frm],
            device_id=(b, to), device_id_type=MESH)

    def edges_copy(to, frm):
        return pltpu.make_async_remote_copy(
            src_ref=group_edge, dst_ref=all_edge.at[frm], send_sem=send2e.at[to], recv_sem=recv2e.at[frm],
            device_id=(b, to), device_id_type=MESH)

    for h in range(1, ngrp):
        @pl.when(h > g)
        def _():
            when(owner(b), lambda: sum_copy(h, g).start())
            edges_copy(h, g).start()
    for h in range(ngrp - 1):
        @pl.when(h < g)
        def _():
            when(owner(b), lambda: sum_copy(g, h).wait_recv())

    def prefix():
        acc = mine[...]
        for h in range(ngrp - 1):
            acc = acc + prior[h]
        whole[b] = acc

    when(owner(b), prefix)

    def whole_copy(to, frm, off):
        return pltpu.make_async_remote_copy(
            src_ref=whole.at[frm], dst_ref=whole.at[frm], send_sem=send3.at[off], recv_sem=recv3.at[frm],
            device_id=(to, g), device_id_type=MESH)

    for off in range(1, nblk):
        when(owner(b), lambda: whole_copy(lax.rem(b + off, nblk), b, off).start())
    for h in range(ngrp - 1):
        @pl.when(h < g)
        def _():
            edges_copy(g, h).wait_recv()
    edge_ref[...] = all_edge[...]
    for off in range(1, nblk):
        frm = lax.rem(b + nblk - off, nblk)
        when(owner(frm), lambda: whole_copy(b, frm, off).wait_recv())
    sum_ref[...] = whole[...]
    for off in range(1, nblk):
        to = lax.rem(b + off, nblk)
        when(owner(to), lambda: slice_copy(to, b, off).wait_send())
        edge_copy(to, b, off).wait_send()
        when(owner(b), lambda: whole_copy(to, b, off).wait_send())
    for h in range(1, ngrp):
        @pl.when(h > g)
        def _():
            when(owner(b), lambda: sum_copy(h, g).wait_send())
            edges_copy(h, g).wait_send()


def lower_inverse(block, out_ref):
    n = TILE // 8
    lane, sub = iota((8, TILE), 1), iota((8, TILE), 0)
    x = [block[8 * r : 8 * r + 8, :] for r in range(n)]

    def rep_lane(v, j):
        return jnp.broadcast_to(v[:, j : j + 1], (8, TILE))

    def rep_row(v, i):
        return jnp.broadcast_to(v[i : i + 1, :], (8, TILE))

    def inverse(p):
        return pl.reciprocal(p, approx=True)

    for q in range(n):
        first = 8 * q
        last = q == n - 1
        cols = [rep_lane(x[q], first + j) for j in range(8)]
        t = {(i, j): rep_row(cols[j], i) for j in range(8) for i in range(j, 8)}
        inside = (lane >= first) & (lane < first + 8)
        aug = jnp.where(inside, jnp.where(lane - first == sub, 1.0, 0.0), x[q])
        y = [rep_row(aug, i) for i in range(8)]
        inv, l, scaled = [None] * 8, {}, [None] * 8
        if not last:
            m = [rep_lane(x[q + 1], first + j) for j in range(8)]
            following = jnp.where(inside, 0.0, x[q + 1])
        for j in range(0, 8, 2):
            a, b, c = t[j, j], t[j + 1, j], t[j + 1, j + 1]
            det = a * c - b * b
            ia, idet = inverse(a), inverse(det)
            ic = a * idet
            inv[j], inv[j + 1] = ia, ic
            rest = range(j + 2, 8)
            for i in range(j + 1, 8):
                l[i, j] = t[i, j] * ia
            e = {i: t[i, j + 1] - l[i, j] * b for i in rest}
            for k in rest:
                for i in range(k, 8):
                    t[i, k] = (t[i, k] - l[i, j] * t[k, j]) - (e[i] * e[k]) * ic
            for i in rest:
                l[i, j + 1] = e[i] * ic
            y[j + 1] = y[j + 1] - l[j + 1, j] * y[j]
            for i in rest:
                y[i] = (y[i] - l[i, j] * y[j]) - l[i, j + 1] * y[j + 1]
            if not last:
                la = m[j] * ia
                em = m[j + 1] - la * b
                lc = em * ic
                for k in rest:
                    m[k] = (m[k] - la * t[k, j]) - lc * e[k]
                following = (following - la * y[j]) - lc * y[j + 1]
            scaled[j] = y[j] * lax.rsqrt(a)
            scaled[j + 1] = y[j + 1] * lax.rsqrt(det * ia)
        rows = scaled[0]
        for i in range(1, 8):
            rows = jnp.where(sub == i, scaled[i], rows)
        out_ref[first : first + 8, :] = jnp.where(lane < first + 8, rows, 0.0)
        if last:
            break
        x[q + 1] = following
        if q + 2 == n:
            continue
        gs = [None] * 8
        for i in range(7, -1, -1):
            acc = y[i] * inv[i]
            for k in range(7, i, -1):
                acc = acc - l[k, i] * gs[k]
            gs[i] = acc
        for r in range(q + 2, n):
            new = jnp.where(inside, 0.0, x[r])
            for j in range(7, -1, -1):
                new = new - rep_lane(x[r], first + j) * gs[j]
            x[r] = new


def fit_kernel(nblk, ngrp, x_ref, lagc_ref, lagr_ref, c_ref, e_ref, fac_ref, coef_ref, res_ref,
               a, ps, pe, tl, vt, dm, miss, u, li, w, v, d, row, li_now):
    b, g = lax.axis_index("blk"), lax.axis_index("grp")
    cols = a.shape[0]
    x = x_ref[...].astype(F32)
    sensors, rows = x.shape
    half = nblk * 8

    ps[...] = jnp.zeros_like(ps)
    pe[...] = jnp.zeros_like(pe)
    tl[...] = jnp.zeros_like(tl)
    dm[...] = jnp.zeros_like(dm)
    miss[...] = jnp.zeros_like(miss)
    lane3 = iota((nblk, 16, TILE), 2)
    left = iota((nblk, 8, TILE), 2) < sensors

    def group_edges(h, carry):
        e = e_ref[h].astype(F32)
        turned = pltpu.roll(e.reshape(nblk * 16, TILE), sensors, 1).reshape(nblk, 16, TILE)
        lo = jnp.where(lane3 < sensors, e, turned)
        hi = jnp.where(lane3 < sensors, turned, e)
        ps[0, 0:8, :] = tl[...]
        if nblk > 1:
            ps[1:, 0:8, :] = lo[: nblk - 1, 8:16, :]
        tl[...] = lo[nblk - 1, 8:16, :]
        pe[:, 0:8, :] = hi[:, 8:16, :]
        head = lo[:, 0:8, :].reshape(half, TILE)
        for i in range(LAGS // 2):
            even, odd = 2 * i + 1, 2 * i + 2
            for ref, at in ((ps, 0), (pe, half)):
                part = jnp.where(left, ref[:, pl.ds(8 - even, 8), :], ref[:, pl.ds(8 - odd, 8), :])
                vt[at : at + half, i * TILE : (i + 1) * TILE] = part.reshape(half, TILE)
        edges = vt[...]
        signed = jnp.where(iota(edges.shape, 0) < half, edges, -edges)
        v16 = edges.astype(BF16)
        dm[...] += dot(signed.T.astype(BF16), v16)
        miss[...] += dot(head.T.astype(BF16), v16[:half])
        return carry

    lax.fori_loop(0, g + 1, group_edges, 0)

    more = jnp.concatenate([miss[0:sensors, :], jnp.zeros((sensors, TILE), F32)], axis=1)
    c = c_ref[...].reshape(sensors, WIDE) + pltpu.roll(more, sensors, 1)
    cm = jnp.where(iota(c.shape, 1) < sensors, 0.5 * c, c)
    cr = pltpu.roll(cm, sensors, 1)
    a[...] = jnp.zeros_like(a)
    for i in range(LAGS):
        base = sensors * (i - i % 2)
        a[sensors * i : sensors * (i + 1), base:cols] = (cr if i % 2 else cm)[:, : cols - base]
    gu = a[:, :cols]
    ridge = (ridge_weight * nblk) * (g + 1).astype(F32)
    eye = jnp.where(iota((cols, cols), 0) == iota((cols, cols), 1), ridge, 0.0)
    gram = gu + gu.T + dm[...] + eye
    cross = jnp.concatenate([c, jnp.zeros_like(c)], axis=0).T[sensors : sensors + cols, :]
    both = jnp.concatenate([gram, cross], axis=1)
    lagc = jnp.concatenate([lagc_ref[...]] * (cols // TILE), axis=1).astype(jnp.int32)
    lagr = lagr_ref[0:1, :].astype(jnp.int32)
    pick = jnp.where(lagc == iota((cols, cols), 1), 1.0, 0.0).astype(BF16)
    pick_t = jnp.where(lagr == iota((cols, cols), 0), 1.0, 0.0).astype(BF16)
    hi, mid, low = split3(both)
    turned = dot(pick, hi) + dot(pick, mid) + dot(pick, low)
    a[:, cols:] = turned[:, cols:]
    hi, mid, low = split3(turned[:, :cols])
    a[:, :cols] = dot(hi, pick_t) + dot(mid, pick_t) + dot(low, pick_t)

    steps = cols // TILE
    u[...] = jnp.zeros_like(u)
    d[...] = a[0:TILE, 0:TILE]
    li[...] = jnp.zeros_like(li)

    def eliminate(k, carry):
        r0 = pl.multiple_of(k * TILE, TILE)
        before = pl.multiple_of(jnp.maximum(k - 1, 0) * TILE, TILE)
        row[...] = a[pl.ds(r0, TILE), :] - exact_dot(u[:, pl.ds(r0, TILE)].T, u[...])
        v[pl.ds(before, TILE), :] = exact_dot(li[pl.ds(before, TILE), :].T, u[pl.ds(before, TILE), :])
        lower_inverse(d[...], li_now)
        now = li_now[...]
        li[pl.ds(r0, TILE), :] = now
        panel = exact_dot(now, row[...])
        panel = jnp.where(iota(panel.shape, 1) >= iota(panel.shape, 0) + r0, panel, 0.0)
        u[pl.ds(r0, TILE), :] = panel

        @pl.when(k < steps - 1)
        def _():
            r1 = pl.multiple_of(r0 + TILE, TILE)
            above = u[:, pl.ds(r1, TILE)]
            d[...] = a[pl.ds(r1, TILE), pl.ds(r1, TILE)] - exact_dot(above.T, above)

        return carry

    lax.fori_loop(0, steps, eliminate, 0)

    end = cols - TILE
    w[end:, :] = exact_dot(li[end:, :].T, u[end:, cols:])
    for k in range(steps - 2, -1, -1):
        at, below = slice(k * TILE, (k + 1) * TILE), (k + 1) * TILE
        w[at, :] = v[at, cols:] - exact_dot(v[at, below:cols], w[below:, :])

    share = cols // nblk
    row0 = pl.multiple_of(b * share, share)
    fac_ref[0] = u[pl.ds(row0, share), :cols] * (1.0 / math.sqrt(rows * nblk))
    coef_ref[0] = w[pl.ds(row0, share), :][:, :sensors]

    hi, mid, low = split3(w[...])
    canon = (dot(pick_t, hi) + dot(pick_t, mid) + dot(pick_t, low)).T[:sensors, :]
    hi, mid, low = split3(canon)
    z = jnp.concatenate([delayed(x, d) for d in range(1, LAGS + 1)], axis=0).astype(BF16)
    fitted = dot(hi, z) + dot(mid, z) + dot(low, z)
    own = vt[pl.ds(pl.multiple_of(b * 8, 8), 8), :]
    own = jnp.concatenate([own, jnp.zeros((TILE - 8, cols), F32)], axis=0).astype(BF16)
    rim = dot_nt(hi, own) + dot_nt(mid, own) + dot_nt(low, own)
    res = x - fitted
    res_ref[0, :, :TILE] = res[:, :TILE] - rim
    res_ref[0, :, TILE:] = res[:, TILE:]


def on_device(nblk, ngrp, signal, lag_table, window_end):
    _, sensors, rows = signal.shape
    cols = lag_table.shape[0]
    ns = min(nblk, sensors // 8)
    per = sensors // ns
    vmem = pl.BlockSpec(memory_space=VMEM)
    smem = pl.BlockSpec(memory_space=pltpu.SMEM)
    dma = pltpu.SemaphoreType.DMA
    sums, edges, x, lagc, lagr = pl.pallas_call(
        functools.partial(share_kernel, nblk, ngrp, ns),
        out_shape=(jax.ShapeDtypeStruct((ns, per, WIDE), F32),
                   jax.ShapeDtypeStruct((ngrp, nblk, 16, TILE), BF16),
                   jax.ShapeDtypeStruct((sensors, rows), BF16),
                   jax.ShapeDtypeStruct((cols, TILE), F32),
                   jax.ShapeDtypeStruct((8, cols), F32)),
        in_specs=[smem, vmem, vmem],
        out_specs=(vmem,) * 5,
        scratch_shapes=[
            VMEM((ns, per, WIDE), F32), VMEM((16, TILE), BF16),
            VMEM((nblk, per, WIDE), F32), VMEM((nblk, 16, TILE), BF16),
            VMEM((ngrp, per, WIDE), F32), VMEM((ngrp, nblk, 16, TILE), BF16),
            VMEM((per, WIDE), F32), VMEM((ns, per, WIDE), F32),
            dma((nblk,)), dma((nblk,)), dma((nblk,)), dma((nblk,)),
            dma((ngrp,)), dma((ngrp,)), dma((ngrp,)), dma((ngrp,)),
            dma((nblk,)), dma((nblk,)),
        ],
        compiler_params=pltpu.CompilerParams(
            collective_id=0, has_side_effects=True, vmem_limit_bytes=32 * 1024 * 1024),
    )(window_end, signal, lag_table.reshape(1, cols))
    half = nblk * 8
    share = cols // nblk
    return pl.pallas_call(
        functools.partial(fit_kernel, nblk, ngrp),
        out_shape=(jax.ShapeDtypeStruct((1, share, cols), F32),
                   jax.ShapeDtypeStruct((1, share, sensors), F32),
                   jax.ShapeDtypeStruct((1, sensors, rows), F32)),
        in_specs=[vmem] * 5,
        out_specs=(vmem, vmem, vmem),
        scratch_shapes=[
            VMEM((cols, WIDE), F32), VMEM((nblk, 16, TILE), F32), VMEM((nblk, 16, TILE), F32),
            VMEM((8, TILE), F32), VMEM((2 * half, cols), F32), VMEM((cols, cols), F32),
            VMEM((TILE, cols), F32), VMEM((cols, WIDE), F32), VMEM((cols, TILE), F32),
            VMEM((cols, TILE), F32), VMEM((cols, WIDE), F32), VMEM((TILE, TILE), F32),
            VMEM((TILE, WIDE), F32), VMEM((TILE, TILE), F32),
        ],
        compiler_params=pltpu.CompilerParams(vmem_limit_bytes=48 * 1024 * 1024),
    )(x, lagc, lagr, sums, edges)


def solution(mesh):
    return jax.shard_map(
        functools.partial(on_device, mesh.shape["blk"], mesh.shape["grp"]),
        mesh=mesh,
        in_specs=(P("grp", None, "blk"), P(), P("grp", "blk")),
        out_specs=(P("grp", "blk", None), P("grp", "blk", None), P("grp", None, "blk")),
        check_vma=False,
    )
```

```python
import functools
import math

import jax
import jax.numpy as jnp
from jax import lax
from jax.experimental import pallas as pl
from jax.experimental.pallas import tpu as pltpu
from jax.sharding import PartitionSpec as P

ridge_weight = 4.0
LAGS = 8
TILE = 128
WIDE = 640
MESH = pl.DeviceIdType.MESH
VMEM = pltpu.VMEM
F32 = jnp.float32
BF16 = jnp.bfloat16


def iota(shape, dim):
    return lax.broadcasted_iota(jnp.int32, shape, dim)


def dot(a, b):
    return jnp.dot(a, b, preferred_element_type=F32)


def dot_nt(a, b):
    return lax.dot_general(a, b, (((1,), (1,)), ((), ())), preferred_element_type=F32)


def exact_dot(a, b):
    return jnp.dot(a, b, precision=lax.Precision.HIGHEST, preferred_element_type=F32)


def split3(x):
    hi = x.astype(BF16)
    rest = x - hi.astype(F32)
    mid = rest.astype(BF16)
    low = (rest - mid.astype(F32)).astype(BF16)
    return hi, mid, low


def delayed(x, delay):
    if delay == 0:
        return x
    return jnp.where(iota(x.shape, 1) < delay, 0.0, pltpu.roll(x, delay, 1))


def moments(x, end):
    sensors, rows = x.shape
    stack = [delayed(x, d) for d in range(LAGS + 1)] + [jnp.zeros_like(x)]
    z = jnp.concatenate(stack, axis=0).astype(BF16)
    xm = jnp.where(iota(x.shape, 1) < end, x, 0.0).astype(BF16)
    c = dot_nt(xm, z)
    row, time = iota((16, rows), 0), iota((16, rows), 1)
    head_tail = jnp.where(row < 8, row, rows - 16 + row)
    last_live = jnp.where(row < 8, -1, end - 16 + row)
    sel_a = jnp.where(time == head_tail, 1.0, 0.0).astype(BF16)
    sel_b = jnp.where(time == last_live, 1.0, 0.0).astype(BF16)
    xl = jnp.concatenate([x, jnp.zeros_like(x)], axis=0).astype(BF16)
    xr = jnp.concatenate([jnp.zeros_like(x), x], axis=0).astype(BF16)
    lagged = z[sensors : sensors * (LAGS + 1), :]
    return lagged, c, (dot_nt(sel_a, xl) + dot_nt(sel_b, xr)).astype(BF16)


def share_kernel(nblk, ngrp, ns, end_ref, x_ref, lag_ref,
                 sum_ref, x_out, pick_ref, pick_t_ref, zp_ref, dm, miss,
                 c_ref, e_ref, pair, acc, part, cls_edge, prior, all_edge, other_edge, mine, whole,
                 ps, pe, tl, vt,
                 send0, recv0, send1, recv1, send1e, recv1e, send2, recv2, send2e, recv2e,
                 send_pe, recv_pe, send3, send3p, recv3):
    b, g = lax.axis_index("blk"), lax.axis_index("grp")
    nz, nso, per = nblk // 2, ns // 2, part.shape[1]
    z, c = b // 2, lax.rem(b, 2)
    partner = 2 * z + 1 - c
    cols = dm.shape[0]
    half = nblk * 8
    owner = (lambda i: True) if nso == nz else (lambda i: i < nso)

    def when(cond, fn):
        if cond is True:
            fn()
        else:
            pl.when(cond)(fn)

    def remote(src, dst, send, recv, blk, grp):
        return pltpu.make_async_remote_copy(
            src_ref=src, dst_ref=dst, send_sem=send, recv_sem=recv,
            device_id=(blk, grp), device_id_type=MESH)

    def ahead(off):
        return lax.rem(z + off, nz)

    def behind(off):
        return lax.rem(z + nz - off, nz)

    prior[...] = jnp.zeros_like(prior)
    all_edge[...] = jnp.zeros_like(all_edge)
    barrier = pltpu.get_barrier_semaphore()
    pl.semaphore_signal(barrier, inc=1, device_id=(partner, g), device_id_type=MESH)
    for off in range(1, nz):
        pl.semaphore_signal(barrier, inc=1, device_id=(2 * ahead(off) + c, g), device_id_type=MESH)
    for off in range(1, ngrp):
        pl.semaphore_signal(barrier, inc=1, device_id=(b, lax.rem(g + off, ngrp)), device_id_type=MESH)
    x = x_ref[0].astype(F32)
    sensors = x.shape[0]
    lagged, moment, e = moments(x, end_ref[0, 0])
    for s in range(ns):
        c_ref[s % 2, s // 2] = moment[s * per : (s + 1) * per, :]
    e_ref[...] = e
    pl.semaphore_wait(barrier, nz + ngrp - 1)

    swap = remote(c_ref.at[1 - c], pair, send0, recv0, partner, g)
    swap.start()

    def edge_copy(to, frm, off):
        return remote(e_ref, cls_edge.at[frm], send1e.at[off], recv1e.at[frm], 2 * to + c, g)

    def slice_copy(to, frm, off):
        return remote(acc.at[to], part.at[frm], send1.at[off], recv1.at[frm], 2 * to + c, g)

    for off in range(1, nz):
        edge_copy(ahead(off), z, off).start()
    cls_edge[z] = e
    swap.wait_recv()
    acc[...] = c_ref[c] + pair[...]
    for off in range(1, nz):
        when(owner(ahead(off)), lambda: slice_copy(ahead(off), z, off).start())
    when(owner(z), lambda: part.__setitem__(z, acc[z]))

    x_out[...] = x_ref[0]
    lag = lag_ref[...]
    lag_col = jnp.broadcast_to(lag.astype(F32), (TILE, cols)).T.astype(jnp.int32)
    lag_col = jnp.concatenate([lag_col] * (cols // TILE), axis=1)
    pick = jnp.where(lag_col == iota((cols, cols), 1), 1.0, 0.0).astype(BF16)
    pick_t = jnp.where(lag == iota((cols, cols), 0), 1.0, 0.0).astype(BF16)
    pick_ref[...] = pick
    pick_t_ref[...] = pick_t
    zp_ref[...] = dot(pick, lagged).astype(BF16)

    for off in range(1, nz):
        when(owner(z), lambda: slice_copy(z, behind(off), off).wait_recv())
        edge_copy(z, behind(off), off).wait_recv()

    def total():
        out = part[0]
        for i in range(1, nz):
            out = out + part[i]
        mine[...] = out

    when(owner(z), total)
    all_edge[g] = cls_edge[...]

    def sum_copy(to, frm):
        return remote(mine, prior.at[frm], send2.at[to], recv2.at[frm], b, to)

    def edges_copy(to, frm):
        return remote(cls_edge, all_edge.at[frm], send2e.at[to], recv2e.at[frm], b, to)

    for h in range(1, ngrp):
        @pl.when(h > g)
        def _():
            when(owner(z), lambda: sum_copy(h, g).start())
            edges_copy(h, g).start()
    for h in range(ngrp - 1):
        @pl.when(h < g)
        def _():
            when(owner(z), lambda: sum_copy(g, h).wait_recv())

    def prefix():
        out = mine[...]
        for h in range(ngrp - 1):
            out = out + prior[h]
        whole[c, z] = out

    when(owner(z), prefix)

    def whole_copy(to, frm, off):
        return remote(whole.at[c, frm], whole.at[c, frm], send3.at[off], recv3.at[c, frm], 2 * to + c, g)

    def pair_copy(cls, frm):
        return remote(whole.at[cls, frm], whole.at[cls, frm], send3p.at[frm], recv3.at[cls, frm], partner, g)

    for off in range(1, nz):
        when(owner(z), lambda: whole_copy(ahead(off), z, off).start())
    when(owner(z), lambda: pair_copy(c, z).start())
    for h in range(ngrp - 1):
        @pl.when(h < g)
        def _():
            edges_copy(g, h).wait_recv()
    swap_edges = remote(all_edge, other_edge, send_pe, recv_pe, partner, g)
    swap_edges.start()
    ps[...] = jnp.zeros_like(ps)
    pe[...] = jnp.zeros_like(pe)
    tl[...] = jnp.zeros_like(tl)
    dm[...] = jnp.zeros_like(dm)
    miss[...] = jnp.zeros_like(miss)
    lane3 = iota((nblk, 16, TILE), 2)
    left = iota((nblk, 8, TILE), 2) < sensors
    swap_edges.wait_recv()

    def group_edges(h, carry):
        ours, theirs = all_edge[h].astype(F32), other_edge[h].astype(F32)
        first = jnp.where(c == 0, ours, theirs)
        second = jnp.where(c == 0, theirs, ours)
        e = jnp.stack([first, second], axis=1).reshape(nblk, 16, TILE)
        turned = pltpu.roll(e.reshape(nblk * 16, TILE), sensors, 1).reshape(nblk, 16, TILE)
        lo = jnp.where(lane3 < sensors, e, turned)
        hi = jnp.where(lane3 < sensors, turned, e)
        ps[0, 0:8, :] = tl[...]
        ps[1:, 0:8, :] = lo[: nblk - 1, 8:16, :]
        tl[...] = lo[nblk - 1, 8:16, :]
        pe[:, 0:8, :] = hi[:, 8:16, :]
        head = lo[:, 0:8, :].reshape(half, TILE)
        for i in range(LAGS // 2):
            even, odd = 2 * i + 1, 2 * i + 2
            for ref, at in ((ps, 0), (pe, half)):
                piece = jnp.where(left, ref[:, pl.ds(8 - even, 8), :], ref[:, pl.ds(8 - odd, 8), :])
                vt[at : at + half, i * TILE : (i + 1) * TILE] = piece.reshape(half, TILE)
        edges = vt[...].astype(BF16)
        turned_edges = dot(edges, pick_t_ref[...])
        signed = jnp.where(iota(turned_edges.shape, 0) < half, turned_edges, -turned_edges)
        dm[...] += dot(signed.T.astype(BF16), turned_edges.astype(BF16))
        miss[...] += dot(head.T.astype(BF16), edges[:half])[:sensors, :]
        return carry

    lax.fori_loop(0, g + 1, group_edges, 0)
    own = vt[pl.ds(pl.multiple_of(b * 8, 8), 8), :]
    own = jnp.concatenate([own, jnp.zeros((TILE - 8, cols), F32)], axis=0).astype(BF16)
    rim = dot(own, pick_t_ref[...]).T
    zp_ref[:, :TILE] = (zp_ref[:, :TILE].astype(F32) + rim).astype(BF16)

    for off in range(1, nz):
        frm = behind(off)

        def forward():
            whole_copy(z, frm, off).wait_recv()
            pair_copy(c, frm).start()

        when(owner(frm), forward)
    for i in range(nso):
        pair_copy(1 - c, i).wait_recv()
    for s in range(ns):
        sum_ref[s * per : (s + 1) * per, :] = whole[s % 2, s // 2]
    swap.wait_send()
    swap_edges.wait_send()
    for i in range(nso):
        pair_copy(c, i).wait_send()
    for off in range(1, nz):
        when(owner(ahead(off)), lambda: slice_copy(ahead(off), z, off).wait_send())
        edge_copy(ahead(off), z, off).wait_send()
        when(owner(z), lambda: whole_copy(ahead(off), z, off).wait_send())
    for h in range(1, ngrp):
        @pl.when(h > g)
        def _():
            when(owner(z), lambda: sum_copy(h, g).wait_send())
            edges_copy(h, g).wait_send()


def lower_inverse(block, out_ref):
    n = TILE // 8
    lane, sub = iota((8, TILE), 1), iota((8, TILE), 0)
    x = [block[8 * r : 8 * r + 8, :] for r in range(n)]

    def rep_lane(v, j):
        return jnp.broadcast_to(v[:, j : j + 1], (8, TILE))

    def rep_row(v, i):
        return jnp.broadcast_to(v[i : i + 1, :], (8, TILE))

    def inverse(p):
        return pl.reciprocal(p, approx=True)

    for q in range(n):
        first = 8 * q
        last = q == n - 1
        cols = [rep_lane(x[q], first + j) for j in range(8)]
        t = {(i, j): rep_row(cols[j], i) for j in range(8) for i in range(j, 8)}
        inside = (lane >= first) & (lane < first + 8)
        aug = jnp.where(inside, jnp.where(lane - first == sub, 1.0, 0.0), x[q])
        y = [rep_row(aug, i) for i in range(8)]
        inv, l, scaled = [None] * 8, {}, [None] * 8
        if not last:
            m = [rep_lane(x[q + 1], first + j) for j in range(8)]
            following = jnp.where(inside, 0.0, x[q + 1])
        for j in range(0, 8, 2):
            a, b, c = t[j, j], t[j + 1, j], t[j + 1, j + 1]
            det = a * c - b * b
            ia, idet = inverse(a), inverse(det)
            ic = a * idet
            inv[j], inv[j + 1] = ia, ic
            rest = range(j + 2, 8)
            for i in range(j + 1, 8):
                l[i, j] = t[i, j] * ia
            e = {i: t[i, j + 1] - l[i, j] * b for i in rest}
            for k in rest:
                for i in range(k, 8):
                    t[i, k] = (t[i, k] - l[i, j] * t[k, j]) - (e[i] * e[k]) * ic
            for i in rest:
                l[i, j + 1] = e[i] * ic
            y[j + 1] = y[j + 1] - l[j + 1, j] * y[j]
            for i in rest:
                y[i] = (y[i] - l[i, j] * y[j]) - l[i, j + 1] * y[j + 1]
            if not last:
                la = m[j] * ia
                em = m[j + 1] - la * b
                lc = em * ic
                for k in rest:
                    m[k] = (m[k] - la * t[k, j]) - lc * e[k]
                following = (following - la * y[j]) - lc * y[j + 1]
            scaled[j] = y[j] * lax.rsqrt(a)
            scaled[j + 1] = y[j + 1] * lax.rsqrt(det * ia)
        rows = scaled[0]
        for i in range(1, 8):
            rows = jnp.where(sub == i, scaled[i], rows)
        out_ref[first : first + 8, :] = jnp.where(lane < first + 8, rows, 0.0)
        if last:
            break
        x[q + 1] = following
        if q + 2 == n:
            continue
        gs = [None] * 8
        for i in range(7, -1, -1):
            acc = y[i] * inv[i]
            for k in range(7, i, -1):
                acc = acc - l[k, i] * gs[k]
            gs[i] = acc
        for r in range(q + 2, n):
            new = jnp.where(inside, 0.0, x[r])
            for j in range(7, -1, -1):
                new = new - rep_lane(x[r], first + j) * gs[j]
            x[r] = new


def fit_kernel(nblk, x_ref, pick_ref, pick_t_ref, zp_ref, dm_ref, miss_ref, c_ref, fac_ref, coef_ref, res_ref,
               a, u, li, w, v, d, row, li_now):
    b, g = lax.axis_index("blk"), lax.axis_index("grp")
    cols = a.shape[0]
    sensors, rows = x_ref.shape
    more = jnp.concatenate([miss_ref[...], jnp.zeros((sensors, TILE), F32)], axis=1)
    c = c_ref[...] + pltpu.roll(more, sensors, 1)
    cm = jnp.where(iota(c.shape, 1) < sensors, 0.5 * c, c)
    cr = pltpu.roll(cm, sensors, 1)
    a[...] = jnp.zeros_like(a)
    for i in range(LAGS):
        base = sensors * (i - i % 2)
        a[sensors * i : sensors * (i + 1), base:cols] = (cr if i % 2 else cm)[:, : cols - base]
    gu = a[:, :cols]
    ridge = (ridge_weight * nblk) * (g + 1).astype(F32)
    eye = jnp.where(iota((cols, cols), 0) == iota((cols, cols), 1), ridge, 0.0)
    gram = gu + gu.T
    cross = jnp.concatenate([c, jnp.zeros_like(c)], axis=0).T[sensors : sensors + cols, :]
    both = jnp.concatenate([gram, cross], axis=1)
    pick, pick_t = pick_ref[...], pick_t_ref[...]
    hi, mid, low = split3(both)
    turned = dot(pick, hi) + dot(pick, mid) + dot(pick, low)
    a[:, cols:] = turned[:, cols:]
    hi, mid, low = split3(turned[:, :cols])
    a[:, :cols] = dot(hi, pick_t) + dot(mid, pick_t) + dot(low, pick_t) + (dm_ref[...] + eye)

    steps = cols // TILE
    u[...] = jnp.zeros_like(u)
    d[...] = a[0:TILE, 0:TILE]
    li[...] = jnp.zeros_like(li)

    def eliminate(k, carry):
        r0 = pl.multiple_of(k * TILE, TILE)
        before = pl.multiple_of(jnp.maximum(k - 1, 0) * TILE, TILE)
        row[...] = a[pl.ds(r0, TILE), :] - exact_dot(u[:, pl.ds(r0, TILE)].T, u[...])
        v[pl.ds(before, TILE), :] = exact_dot(li[pl.ds(before, TILE), :].T, u[pl.ds(before, TILE), :])
        lower_inverse(d[...], li_now)
        now = li_now[...]
        li[pl.ds(r0, TILE), :] = now
        panel = exact_dot(now, row[...])
        panel = jnp.where(iota(panel.shape, 1) >= iota(panel.shape, 0) + r0, panel, 0.0)
        u[pl.ds(r0, TILE), :] = panel

        @pl.when(k < steps - 1)
        def _():
            r1 = pl.multiple_of(r0 + TILE, TILE)
            above = u[:, pl.ds(r1, TILE)]
            d[...] = a[pl.ds(r1, TILE), pl.ds(r1, TILE)] - exact_dot(above.T, above)

        return carry

    lax.fori_loop(0, steps, eliminate, 0)

    end = cols - TILE
    w[end:, :] = exact_dot(li[end:, :].T, u[end:, cols:])
    for k in range(steps - 2, -1, -1):
        at, below = slice(k * TILE, (k + 1) * TILE), (k + 1) * TILE
        w[at, :] = v[at, cols:] - exact_dot(v[at, below:cols], w[below:, :])

    share = cols // nblk
    row0 = pl.multiple_of(b * share, share)
    fac_ref[0] = u[pl.ds(row0, share), :cols] * (1.0 / math.sqrt(rows * nblk))
    coef_ref[0] = w[pl.ds(row0, share), :][:, :sensors]

    hi, mid, low = split3(w[...].T[:sensors, :])
    zp = zp_ref[...]
    res_ref[0] = x_ref[...].astype(F32) - (dot(hi, zp) + dot(mid, zp) + dot(low, zp))


def on_device(nblk, ngrp, signal, lag_table, window_end):
    _, sensors, rows = signal.shape
    cols = lag_table.shape[0]
    ns = min(nblk, sensors // 8)
    per = sensors // ns
    vmem = pl.BlockSpec(memory_space=VMEM)
    smem = pl.BlockSpec(memory_space=pltpu.SMEM)
    dma = pltpu.SemaphoreType.DMA
    half = nblk * 8
    nz, nso = nblk // 2, ns // 2
    share = cols // nblk
    sums, x, pick, pick_t, zp, dm, miss = pl.pallas_call(
        functools.partial(share_kernel, nblk, ngrp, ns),
        out_shape=(jax.ShapeDtypeStruct((sensors, WIDE), F32),
                   jax.ShapeDtypeStruct((sensors, rows), BF16),
                   jax.ShapeDtypeStruct((cols, cols), BF16),
                   jax.ShapeDtypeStruct((cols, cols), BF16),
                   jax.ShapeDtypeStruct((cols, rows), BF16),
                   jax.ShapeDtypeStruct((cols, cols), F32),
                   jax.ShapeDtypeStruct((sensors, cols), F32)),
        in_specs=[smem, vmem, vmem],
        out_specs=(vmem,) * 7,
        scratch_shapes=[
            VMEM((2, nso, per, WIDE), F32), VMEM((16, TILE), BF16),
            VMEM((nso, per, WIDE), F32), VMEM((nso, per, WIDE), F32),
            VMEM((nz, per, WIDE), F32), VMEM((nz, 16, TILE), BF16),
            VMEM((ngrp, per, WIDE), F32), VMEM((ngrp, nz, 16, TILE), BF16),
            VMEM((ngrp, nz, 16, TILE), BF16),
            VMEM((per, WIDE), F32), VMEM((2, nso, per, WIDE), F32),
            VMEM((nblk, 16, TILE), F32), VMEM((nblk, 16, TILE), F32), VMEM((8, TILE), F32),
            VMEM((2 * half, cols), F32),
            dma, dma, dma((nz,)), dma((nz,)), dma((nz,)), dma((nz,)),
            dma((ngrp,)), dma((ngrp,)), dma((ngrp,)), dma((ngrp,)),
            dma, dma, dma((nz,)), dma((nso,)), dma((2, nso)),
        ],
        compiler_params=pltpu.CompilerParams(
            collective_id=0, has_side_effects=True, vmem_limit_bytes=32 * 1024 * 1024),
    )(window_end, signal, lag_table.reshape(1, cols))
    return pl.pallas_call(
        functools.partial(fit_kernel, nblk),
        out_shape=(jax.ShapeDtypeStruct((1, share, cols), F32),
                   jax.ShapeDtypeStruct((1, share, sensors), F32),
                   jax.ShapeDtypeStruct((1, sensors, rows), F32)),
        in_specs=[vmem] * 7,
        out_specs=(vmem, vmem, vmem),
        scratch_shapes=[
            VMEM((cols, WIDE), F32), VMEM((cols, WIDE), F32), VMEM((cols, TILE), F32),
            VMEM((cols, TILE), F32), VMEM((cols, WIDE), F32), VMEM((TILE, TILE), F32),
            VMEM((TILE, WIDE), F32), VMEM((TILE, TILE), F32),
        ],
        compiler_params=pltpu.CompilerParams(vmem_limit_bytes=40 * 1024 * 1024),
    )(x, pick, pick_t, zp, dm, miss, sums)


def solution(mesh):
    return jax.shard_map(
        functools.partial(on_device, mesh.shape["blk"], mesh.shape["grp"]),
        mesh=mesh,
        in_specs=(P("grp", None, "blk"), P(), P("grp", "blk")),
        out_specs=(P("grp", "blk", None), P("grp", "blk", None), P("grp", None, "blk")),
        check_vma=False,
    )
```

```python
import functools
import math

import jax
import jax.numpy as jnp
from jax import lax
from jax.experimental import pallas as pl
from jax.experimental.pallas import tpu as pltpu
from jax.sharding import PartitionSpec as P

ridge_weight = 4.0
LAGS = 8
TILE = 128
WIDE = 640
MESH = pl.DeviceIdType.MESH
VMEM = pltpu.VMEM
F32 = jnp.float32
BF16 = jnp.bfloat16


def iota(shape, dim):
    return lax.broadcasted_iota(jnp.int32, shape, dim)


def dot(a, b):
    return jnp.dot(a, b, preferred_element_type=F32)


def dot_nt(a, b):
    return lax.dot_general(a, b, (((1,), (1,)), ((), ())), preferred_element_type=F32)


def exact_dot(a, b):
    return jnp.dot(a, b, precision=lax.Precision.HIGHEST, preferred_element_type=F32)


def split3(x):
    hi = x.astype(BF16)
    rest = x - hi.astype(F32)
    mid = rest.astype(BF16)
    low = (rest - mid.astype(F32)).astype(BF16)
    return hi, mid, low


def delayed(x, delay):
    if delay == 0:
        return x
    return jnp.where(iota(x.shape, 1) < delay, 0.0, pltpu.roll(x, delay, 1))


def moments(x, end):
    sensors, rows = x.shape
    stack = [delayed(x, d) for d in range(LAGS + 1)] + [jnp.zeros_like(x)]
    z = jnp.concatenate(stack, axis=0).astype(BF16)
    xm = jnp.where(iota(x.shape, 1) < end, x, 0.0).astype(BF16)
    c = dot_nt(xm, z)
    row, time = iota((16, rows), 0), iota((16, rows), 1)
    head_tail = jnp.where(row < 8, row, rows - 16 + row)
    last_live = jnp.where(row < 8, -1, end - 16 + row)
    sel_a = jnp.where(time == head_tail, 1.0, 0.0).astype(BF16)
    sel_b = jnp.where(time == last_live, 1.0, 0.0).astype(BF16)
    xl = jnp.concatenate([x, jnp.zeros_like(x)], axis=0).astype(BF16)
    xr = jnp.concatenate([jnp.zeros_like(x), x], axis=0).astype(BF16)
    lagged = z[sensors : sensors * (LAGS + 1), :]
    return lagged, c, (dot_nt(sel_a, xl) + dot_nt(sel_b, xr)).astype(BF16)


def share_kernel(nblk, ngrp, ns, end_hbm, x_hbm, lag_hbm,
                 sum_ref, x_out, pick_ref, pick_t_ref, zp_ref, dm, miss,
                 c_ref, e_ref, pair, acc, part, cls_edge, prior, all_edge, other_edge, mine, whole,
                 ps, pe, tl, vt,
                 send0, recv0, send1, recv1, send1e, recv1e, send2, recv2, send2e, recv2e,
                 send_pe, recv_pe, send3, send3p, recv3, end_ref, lag_ref, x_ref, fetch):
    b, g = lax.axis_index("blk"), lax.axis_index("grp")
    nz, nso, per = nblk // 2, ns // 2, part.shape[1]
    z, c = b // 2, lax.rem(b, 2)
    partner = 2 * z + 1 - c
    cols = dm.shape[0]
    half = nblk * 8
    owner = (lambda i: True) if nso == nz else (lambda i: i < nso)

    def when(cond, fn):
        if cond is True:
            fn()
        else:
            pl.when(cond)(fn)

    def remote(src, dst, send, recv, blk, grp):
        return pltpu.make_async_remote_copy(
            src_ref=src, dst_ref=dst, send_sem=send, recv_sem=recv,
            device_id=(blk, grp), device_id_type=MESH)

    def ahead(off):
        return lax.rem(z + off, nz)

    def behind(off):
        return lax.rem(z + nz - off, nz)

    loads = [pltpu.make_async_copy(src, dst, fetch.at[i])
             for i, (src, dst) in enumerate(((x_hbm, x_ref), (end_hbm, end_ref), (lag_hbm, lag_ref)))]
    for load in loads:
        load.start()
    prior[...] = jnp.zeros_like(prior)
    all_edge[...] = jnp.zeros_like(all_edge)
    barrier = pltpu.get_barrier_semaphore()
    pl.semaphore_signal(barrier, inc=1, device_id=(partner, g), device_id_type=MESH)
    for off in range(1, nz):
        pl.semaphore_signal(barrier, inc=1, device_id=(2 * ahead(off) + c, g), device_id_type=MESH)
    for off in range(1, ngrp):
        pl.semaphore_signal(barrier, inc=1, device_id=(b, lax.rem(g + off, ngrp)), device_id_type=MESH)
    for load in loads:
        load.wait()
    x = x_ref[0].astype(F32)
    sensors = x.shape[0]
    lagged, moment, e = moments(x, end_ref[0, 0])
    for s in range(ns):
        c_ref[s % 2, s // 2] = moment[s * per : (s + 1) * per, :]
    e_ref[...] = e
    pl.semaphore_wait(barrier, nz + ngrp - 1)

    swap = remote(c_ref.at[1 - c], pair, send0, recv0, partner, g)
    swap.start()

    def edge_copy(to, frm, off):
        return remote(e_ref, cls_edge.at[frm], send1e.at[off], recv1e.at[frm], 2 * to + c, g)

    def slice_copy(to, frm, off):
        return remote(acc.at[to], part.at[frm], send1.at[off], recv1.at[frm], 2 * to + c, g)

    for off in range(1, nz):
        edge_copy(ahead(off), z, off).start()
    cls_edge[z] = e
    swap.wait_recv()
    acc[...] = c_ref[c] + pair[...]
    for off in range(1, nz):
        when(owner(ahead(off)), lambda: slice_copy(ahead(off), z, off).start())
    when(owner(z), lambda: part.__setitem__(z, acc[z]))

    x_out[...] = x_ref[0]
    lag = lag_ref[...]
    lag_col = jnp.broadcast_to(lag.astype(F32), (TILE, cols)).T.astype(jnp.int32)
    lag_col = jnp.concatenate([lag_col] * (cols // TILE), axis=1)
    pick = jnp.where(lag_col == iota((cols, cols), 1), 1.0, 0.0).astype(BF16)
    pick_t = jnp.where(lag == iota((cols, cols), 0), 1.0, 0.0).astype(BF16)
    pick_ref[...] = pick
    pick_t_ref[...] = pick_t
    zp_ref[...] = dot(pick, lagged).astype(BF16)

    for off in range(1, nz):
        when(owner(z), lambda: slice_copy(z, behind(off), off).wait_recv())
        edge_copy(z, behind(off), off).wait_recv()

    def total():
        out = part[0]
        for i in range(1, nz):
            out = out + part[i]
        mine[...] = out

    when(owner(z), total)
    all_edge[g] = cls_edge[...]

    def sum_copy(to, frm):
        return remote(mine, prior.at[frm], send2.at[to], recv2.at[frm], b, to)

    def edges_copy(to, frm):
        return remote(cls_edge, all_edge.at[frm], send2e.at[to], recv2e.at[frm], b, to)

    for h in range(1, ngrp):
        @pl.when(h > g)
        def _():
            when(owner(z), lambda: sum_copy(h, g).start())
            edges_copy(h, g).start()
    for h in range(ngrp - 1):
        @pl.when(h < g)
        def _():
            when(owner(z), lambda: sum_copy(g, h).wait_recv())

    def prefix():
        out = mine[...]
        for h in range(ngrp - 1):
            out = out + prior[h]
        whole[c, z] = out

    when(owner(z), prefix)

    def whole_copy(to, frm, off):
        return remote(whole.at[c, frm], whole.at[c, frm], send3.at[off], recv3.at[c, frm], 2 * to + c, g)

    def pair_copy(cls, frm):
        return remote(whole.at[cls, frm], whole.at[cls, frm], send3p.at[frm], recv3.at[cls, frm], partner, g)

    for off in range(1, nz):
        when(owner(z), lambda: whole_copy(ahead(off), z, off).start())
    when(owner(z), lambda: pair_copy(c, z).start())
    for h in range(ngrp - 1):
        @pl.when(h < g)
        def _():
            edges_copy(g, h).wait_recv()
    swap_edges = remote(all_edge, other_edge, send_pe, recv_pe, partner, g)
    swap_edges.start()
    ps[...] = jnp.zeros_like(ps)
    pe[...] = jnp.zeros_like(pe)
    tl[...] = jnp.zeros_like(tl)
    dm[...] = jnp.zeros_like(dm)
    miss[...] = jnp.zeros_like(miss)
    lane3 = iota((nblk, 16, TILE), 2)
    left = iota((nblk, 8, TILE), 2) < sensors
    swap_edges.wait_recv()

    def group_edges(h, carry):
        ours, theirs = all_edge[h].astype(F32), other_edge[h].astype(F32)
        first = jnp.where(c == 0, ours, theirs)
        second = jnp.where(c == 0, theirs, ours)
        e = jnp.stack([first, second], axis=1).reshape(nblk, 16, TILE)
        turned = pltpu.roll(e.reshape(nblk * 16, TILE), sensors, 1).reshape(nblk, 16, TILE)
        lo = jnp.where(lane3 < sensors, e, turned)
        hi = jnp.where(lane3 < sensors, turned, e)
        ps[0, 0:8, :] = tl[...]
        ps[1:, 0:8, :] = lo[: nblk - 1, 8:16, :]
        tl[...] = lo[nblk - 1, 8:16, :]
        pe[:, 0:8, :] = hi[:, 8:16, :]
        head = lo[:, 0:8, :].reshape(half, TILE)
        for i in range(LAGS // 2):
            even, odd = 2 * i + 1, 2 * i + 2
            for ref, at in ((ps, 0), (pe, half)):
                piece = jnp.where(left, ref[:, pl.ds(8 - even, 8), :], ref[:, pl.ds(8 - odd, 8), :])
                vt[at : at + half, i * TILE : (i + 1) * TILE] = piece.reshape(half, TILE)
        edges = vt[...].astype(BF16)
        turned_edges = dot(edges, pick_t_ref[...])
        signed = jnp.where(iota(turned_edges.shape, 0) < half, turned_edges, -turned_edges)
        dm[...] += dot(signed.T.astype(BF16), turned_edges.astype(BF16))
        miss[...] += dot(head.T.astype(BF16), edges[:half])[:sensors, :]
        return carry

    lax.fori_loop(0, g + 1, group_edges, 0)
    own = vt[pl.ds(pl.multiple_of(b * 8, 8), 8), :]
    own = jnp.concatenate([own, jnp.zeros((TILE - 8, cols), F32)], axis=0).astype(BF16)
    rim = dot(own, pick_t_ref[...]).T
    zp_ref[:, :TILE] = (zp_ref[:, :TILE].astype(F32) + rim).astype(BF16)

    for off in range(1, nz):
        frm = behind(off)

        def forward():
            whole_copy(z, frm, off).wait_recv()
            pair_copy(c, frm).start()

        when(owner(frm), forward)
    for i in range(nso):
        pair_copy(1 - c, i).wait_recv()
    for s in range(ns):
        sum_ref[s * per : (s + 1) * per, :] = whole[s % 2, s // 2]
    swap.wait_send()
    swap_edges.wait_send()
    for i in range(nso):
        pair_copy(c, i).wait_send()
    for off in range(1, nz):
        when(owner(ahead(off)), lambda: slice_copy(ahead(off), z, off).wait_send())
        edge_copy(ahead(off), z, off).wait_send()
        when(owner(z), lambda: whole_copy(ahead(off), z, off).wait_send())
    for h in range(1, ngrp):
        @pl.when(h > g)
        def _():
            when(owner(z), lambda: sum_copy(h, g).wait_send())
            edges_copy(h, g).wait_send()


def lower_inverse(block, out_ref):
    n = TILE // 8
    lane, sub = iota((8, TILE), 1), iota((8, TILE), 0)
    x = [block[8 * r : 8 * r + 8, :] for r in range(n)]

    def rep_lane(v, j):
        return jnp.broadcast_to(v[:, j : j + 1], (8, TILE))

    def rep_row(v, i):
        return jnp.broadcast_to(v[i : i + 1, :], (8, TILE))

    def inverse(p):
        return pl.reciprocal(p, approx=True)

    for q in range(n):
        first = 8 * q
        last = q == n - 1
        cols = [rep_lane(x[q], first + j) for j in range(8)]
        t = {(i, j): rep_row(cols[j], i) for j in range(8) for i in range(j, 8)}
        inside = (lane >= first) & (lane < first + 8)
        aug = jnp.where(inside, jnp.where(lane - first == sub, 1.0, 0.0), x[q])
        y = [rep_row(aug, i) for i in range(8)]
        inv, l, scaled = [None] * 8, {}, [None] * 8
        if not last:
            m = [rep_lane(x[q + 1], first + j) for j in range(8)]
            following = jnp.where(inside, 0.0, x[q + 1])
        for j in range(0, 8, 2):
            a, b, c = t[j, j], t[j + 1, j], t[j + 1, j + 1]
            det = a * c - b * b
            ia, idet = inverse(a), inverse(det)
            ic = a * idet
            inv[j], inv[j + 1] = ia, ic
            rest = range(j + 2, 8)
            for i in range(j + 1, 8):
                l[i, j] = t[i, j] * ia
            e = {i: t[i, j + 1] - l[i, j] * b for i in rest}
            for k in rest:
                for i in range(k, 8):
                    t[i, k] = (t[i, k] - l[i, j] * t[k, j]) - (e[i] * e[k]) * ic
            for i in rest:
                l[i, j + 1] = e[i] * ic
            y[j + 1] = y[j + 1] - l[j + 1, j] * y[j]
            for i in rest:
                y[i] = (y[i] - l[i, j] * y[j]) - l[i, j + 1] * y[j + 1]
            if not last:
                la = m[j] * ia
                em = m[j + 1] - la * b
                lc = em * ic
                for k in rest:
                    m[k] = (m[k] - la * t[k, j]) - lc * e[k]
                following = (following - la * y[j]) - lc * y[j + 1]
            scaled[j] = y[j] * lax.rsqrt(a)
            scaled[j + 1] = y[j + 1] * lax.rsqrt(det * ia)
        rows = scaled[0]
        for i in range(1, 8):
            rows = jnp.where(sub == i, scaled[i], rows)
        out_ref[first : first + 8, :] = jnp.where(lane < first + 8, rows, 0.0)
        if last:
            break
        x[q + 1] = following
        if q + 2 == n:
            continue
        gs = [None] * 8
        for i in range(7, -1, -1):
            acc = y[i] * inv[i]
            for k in range(7, i, -1):
                acc = acc - l[k, i] * gs[k]
            gs[i] = acc
        for r in range(q + 2, n):
            new = jnp.where(inside, 0.0, x[r])
            for j in range(7, -1, -1):
                new = new - rep_lane(x[r], first + j) * gs[j]
            x[r] = new


def fit_kernel(nblk, x_ref, pick_ref, pick_t_ref, zp_ref, dm_ref, miss_ref, c_ref, fac_ref, coef_ref, res_ref,
               a, u, li, w, v, d, row, li_now, parts, dn):
    b, g = lax.axis_index("blk"), lax.axis_index("grp")
    cols = a.shape[0]
    sensors, rows = x_ref.shape
    more = jnp.concatenate([miss_ref[...], jnp.zeros((sensors, TILE), F32)], axis=1)
    c = c_ref[...] + pltpu.roll(more, sensors, 1)
    cm = jnp.where(iota(c.shape, 1) < sensors, 0.5 * c, c)
    cr = pltpu.roll(cm, sensors, 1)
    a[...] = jnp.zeros_like(a)
    for i in range(LAGS):
        base = sensors * (i - i % 2)
        a[sensors * i : sensors * (i + 1), base:cols] = (cr if i % 2 else cm)[:, : cols - base]
    gu = a[:, :cols]
    ridge = (ridge_weight * nblk) * (g + 1).astype(F32)
    gram = gu + gu.T
    cross = jnp.concatenate([c, jnp.zeros_like(c)], axis=0).T[sensors : sensors + cols, :]
    both = jnp.concatenate([gram, cross], axis=1)
    for i, piece in enumerate(split3(both)):
        parts[i] = piece

    def assemble(r):
        pick = pick_ref[pl.ds(r, TILE), :]
        turned = dot(pick, parts[0]) + dot(pick, parts[1]) + dot(pick, parts[2])
        hi, mid, low = split3(turned[:, :cols])
        pick_t = pick_t_ref[...]
        eye = jnp.where(iota((TILE, cols), 0) + r == iota((TILE, cols), 1), ridge, 0.0)
        gram = dot(hi, pick_t) + dot(mid, pick_t) + dot(low, pick_t) + (dm_ref[pl.ds(r, TILE), :] + eye)
        a[pl.ds(r, TILE), :] = jnp.concatenate([gram, turned[:, cols:]], axis=1)

    steps = cols // TILE
    u[...] = jnp.zeros_like(u)
    li[...] = jnp.zeros_like(li)
    assemble(0)
    d[...] = a[0:TILE, 0:TILE]

    def eliminate(k, carry):
        r0 = pl.multiple_of(k * TILE, TILE)
        before = pl.multiple_of(jnp.maximum(k - 1, 0) * TILE, TILE)
        r1 = pl.multiple_of(jnp.minimum(k + 1, steps - 1) * TILE, TILE)
        row[...] = a[pl.ds(r0, TILE), :] - exact_dot(u[:, pl.ds(r0, TILE)].T, u[...])
        v[pl.ds(before, TILE), :] = exact_dot(li[pl.ds(before, TILE), :].T, u[pl.ds(before, TILE), :])
        above = u[:, pl.ds(r1, TILE)]
        dn[...] = exact_dot(above.T, above)
        assemble(r1)
        lower_inverse(d[...], li_now)
        now = li_now[...]
        li[pl.ds(r0, TILE), :] = now
        panel = exact_dot(now, row[...])
        panel = jnp.where(iota(panel.shape, 1) >= iota(panel.shape, 0) + r0, panel, 0.0)
        u[pl.ds(r0, TILE), :] = panel
        new = u[pl.ds(r0, TILE), pl.ds(r1, TILE)]
        d[...] = (a[pl.ds(r1, TILE), pl.ds(r1, TILE)] - dn[...]) - exact_dot(new.T, new)
        return carry

    lax.fori_loop(0, steps, eliminate, 0)

    end = cols - TILE
    w[end:, :] = exact_dot(li[end:, :].T, u[end:, cols:])
    for k in range(steps - 2, -1, -1):
        at, below = slice(k * TILE, (k + 1) * TILE), (k + 1) * TILE
        w[at, :] = v[at, cols:] - exact_dot(v[at, below:cols], w[below:, :])

    share = cols // nblk
    row0 = pl.multiple_of(b * share, share)
    fac_ref[0] = u[pl.ds(row0, share), :cols] * (1.0 / math.sqrt(rows * nblk))
    coef_ref[0] = w[pl.ds(row0, share), :][:, :sensors]

    hi, mid, low = split3(w[...].T[:sensors, :])
    zp = zp_ref[...]
    res_ref[0] = x_ref[...].astype(F32) - (dot(hi, zp) + dot(mid, zp) + dot(low, zp))


def on_device(nblk, ngrp, signal, lag_table, window_end):
    _, sensors, rows = signal.shape
    cols = lag_table.shape[0]
    ns = min(nblk, sensors // 8)
    per = sensors // ns
    vmem = pl.BlockSpec(memory_space=VMEM)
    dma = pltpu.SemaphoreType.DMA
    half = nblk * 8
    nz, nso = nblk // 2, ns // 2
    share = cols // nblk
    sums, x, pick, pick_t, zp, dm, miss = pl.pallas_call(
        functools.partial(share_kernel, nblk, ngrp, ns),
        out_shape=(jax.ShapeDtypeStruct((sensors, WIDE), F32),
                   jax.ShapeDtypeStruct((sensors, rows), BF16),
                   jax.ShapeDtypeStruct((cols, cols), BF16),
                   jax.ShapeDtypeStruct((cols, cols), BF16),
                   jax.ShapeDtypeStruct((cols, rows), BF16),
                   jax.ShapeDtypeStruct((cols, cols), F32),
                   jax.ShapeDtypeStruct((sensors, cols), F32)),
        in_specs=[pl.BlockSpec(memory_space=pltpu.HBM)] * 3,
        out_specs=(vmem,) * 7,
        scratch_shapes=[
            VMEM((2, nso, per, WIDE), F32), VMEM((16, TILE), BF16),
            VMEM((nso, per, WIDE), F32), VMEM((nso, per, WIDE), F32),
            VMEM((nz, per, WIDE), F32), VMEM((nz, 16, TILE), BF16),
            VMEM((ngrp, per, WIDE), F32), VMEM((ngrp, nz, 16, TILE), BF16),
            VMEM((ngrp, nz, 16, TILE), BF16),
            VMEM((per, WIDE), F32), VMEM((2, nso, per, WIDE), F32),
            VMEM((nblk, 16, TILE), F32), VMEM((nblk, 16, TILE), F32), VMEM((8, TILE), F32),
            VMEM((2 * half, cols), F32),
            dma, dma, dma((nz,)), dma((nz,)), dma((nz,)), dma((nz,)),
            dma((ngrp,)), dma((ngrp,)), dma((ngrp,)), dma((ngrp,)),
            dma, dma, dma((nz,)), dma((nso,)), dma((2, nso)),
            pltpu.SMEM((1, 1), jnp.int32), VMEM((1, cols), jnp.int32), VMEM((1, sensors, rows), BF16), dma((3,)),
        ],
        compiler_params=pltpu.CompilerParams(
            collective_id=0, has_side_effects=True, vmem_limit_bytes=32 * 1024 * 1024),
    )(window_end, signal, lag_table.reshape(1, cols))
    return pl.pallas_call(
        functools.partial(fit_kernel, nblk),
        out_shape=(jax.ShapeDtypeStruct((1, share, cols), F32),
                   jax.ShapeDtypeStruct((1, share, sensors), F32),
                   jax.ShapeDtypeStruct((1, sensors, rows), F32)),
        in_specs=[vmem] * 7,
        out_specs=(vmem, vmem, vmem),
        scratch_shapes=[
            VMEM((cols, WIDE), F32), VMEM((cols, WIDE), F32), VMEM((cols, TILE), F32),
            VMEM((cols, TILE), F32), VMEM((cols, WIDE), F32), VMEM((TILE, TILE), F32),
            VMEM((TILE, WIDE), F32), VMEM((TILE, TILE), F32), VMEM((3, cols, WIDE), BF16), VMEM((TILE, TILE), F32),
        ],
        compiler_params=pltpu.CompilerParams(vmem_limit_bytes=40 * 1024 * 1024),
    )(x, pick, pick_t, zp, dm, miss, sums)


def solution(mesh):
    return jax.shard_map(
        functools.partial(on_device, mesh.shape["blk"], mesh.shape["grp"]),
        mesh=mesh,
        in_specs=(P("grp", None, "blk"), P(), P("grp", "blk")),
        out_specs=(P("grp", "blk", None), P("grp", "blk", None), P("grp", None, "blk")),
        check_vma=False,
    )
```

```python
import functools
import math

import jax
import jax.numpy as jnp
from jax import lax
from jax.experimental import pallas as pl
from jax.experimental.pallas import tpu as pltpu
from jax.sharding import PartitionSpec as P

ridge_weight = 4.0
LAGS = 8
TILE = 128
WIDE = 640
MESH = pl.DeviceIdType.MESH
VMEM = pltpu.VMEM
F32 = jnp.float32
BF16 = jnp.bfloat16


def iota(shape, dim):
    return lax.broadcasted_iota(jnp.int32, shape, dim)


def dot(a, b):
    return jnp.dot(a, b, preferred_element_type=F32)


def dot_nt(a, b):
    return lax.dot_general(a, b, (((1,), (1,)), ((), ())), preferred_element_type=F32)


def exact_dot(a, b):
    return jnp.dot(a, b, precision=lax.Precision.HIGHEST, preferred_element_type=F32)


def split3(x):
    hi = x.astype(BF16)
    rest = x - hi.astype(F32)
    mid = rest.astype(BF16)
    low = (rest - mid.astype(F32)).astype(BF16)
    return hi, mid, low


def delayed(x, delay):
    if delay == 0:
        return x
    return jnp.where(iota(x.shape, 1) < delay, 0.0, pltpu.roll(x, delay, 1))


def moments(x, end):
    sensors, rows = x.shape
    stack = [delayed(x, d) for d in range(LAGS + 1)] + [jnp.zeros_like(x)]
    z = jnp.concatenate(stack, axis=0).astype(BF16)
    xm = jnp.where(iota(x.shape, 1) < end, x, 0.0).astype(BF16)
    c = dot_nt(xm, z)
    row, time = iota((16, rows), 0), iota((16, rows), 1)
    head_tail = jnp.where(row < 8, row, rows - 16 + row)
    last_live = jnp.where(row < 8, -1, end - 16 + row)
    sel_a = jnp.where(time == head_tail, 1.0, 0.0).astype(BF16)
    sel_b = jnp.where(time == last_live, 1.0, 0.0).astype(BF16)
    xl = jnp.concatenate([x, jnp.zeros_like(x)], axis=0).astype(BF16)
    xr = jnp.concatenate([jnp.zeros_like(x), x], axis=0).astype(BF16)
    lagged = z[sensors : sensors * (LAGS + 1), :]
    return lagged, c, (dot_nt(sel_a, xl) + dot_nt(sel_b, xr)).astype(BF16)


def share_kernel(nblk, ngrp, ns, end_hbm, x_hbm, lag_hbm,
                 sum_ref, x_out, pick_ref, pick_t_ref, zp_ref, dm, miss,
                 c_ref, e_ref, pair, acc, part, cls_edge, prior, all_edge, other_edge, mine, whole,
                 ps, pe, tl, vt,
                 send0, recv0, send1, recv1, send1e, recv1e, send2, recv2, send2e, recv2e,
                 send_pe, recv_pe, send3, send3p, recv3, end_ref, lag_ref, x_ref, fetch):
    b, g = lax.axis_index("blk"), lax.axis_index("grp")
    nz, nso, per = nblk // 2, ns // 2, part.shape[1]
    z, c = b // 2, lax.rem(b, 2)
    partner = 2 * z + 1 - c
    cols = dm.shape[0]
    half = nblk * 8
    owner = (lambda i: True) if nso == nz else (lambda i: i < nso)

    def when(cond, fn):
        if cond is True:
            fn()
        else:
            pl.when(cond)(fn)

    def remote(src, dst, send, recv, blk, grp):
        return pltpu.make_async_remote_copy(
            src_ref=src, dst_ref=dst, send_sem=send, recv_sem=recv,
            device_id=(blk, grp), device_id_type=MESH)

    def ahead(off):
        return lax.rem(z + off, nz)

    def behind(off):
        return lax.rem(z + nz - off, nz)

    loads = [pltpu.make_async_copy(src, dst, fetch.at[i])
             for i, (src, dst) in enumerate(((x_hbm, x_ref), (end_hbm, end_ref), (lag_hbm, lag_ref)))]
    for load in loads:
        load.start()
    prior[...] = jnp.zeros_like(prior)
    all_edge[...] = jnp.zeros_like(all_edge)
    barrier = pltpu.get_barrier_semaphore()
    pl.semaphore_signal(barrier, inc=1, device_id=(partner, g), device_id_type=MESH)
    for off in range(1, nz):
        pl.semaphore_signal(barrier, inc=1, device_id=(2 * ahead(off) + c, g), device_id_type=MESH)
    for off in range(1, ngrp):
        pl.semaphore_signal(barrier, inc=1, device_id=(b, lax.rem(g + off, ngrp)), device_id_type=MESH)
    for load in loads:
        load.wait()
    x = x_ref[0].astype(F32)
    sensors = x.shape[0]
    lagged, moment, e = moments(x, end_ref[0, 0])
    for s in range(ns):
        c_ref[s % 2, s // 2] = moment[s * per : (s + 1) * per, :]
    e_ref[...] = e
    pl.semaphore_wait(barrier, nz + ngrp - 1)

    swap = remote(c_ref.at[1 - c], pair, send0, recv0, partner, g)
    swap.start()

    def edge_copy(to, frm, off):
        return remote(e_ref, cls_edge.at[frm], send1e.at[off], recv1e.at[frm], 2 * to + c, g)

    def slice_copy(to, frm, off):
        return remote(acc.at[to], part.at[frm], send1.at[off], recv1.at[frm], 2 * to + c, g)

    for off in range(1, nz):
        edge_copy(ahead(off), z, off).start()
    cls_edge[z] = e
    swap.wait_recv()
    acc[...] = c_ref[c] + pair[...]
    for off in range(1, nz):
        when(owner(ahead(off)), lambda: slice_copy(ahead(off), z, off).start())
    when(owner(z), lambda: part.__setitem__(z, acc[z]))

    x_out[...] = x_ref[0]
    lag = lag_ref[...]
    lag_col = jnp.broadcast_to(lag.astype(F32), (TILE, cols)).T.astype(jnp.int32)
    lag_col = jnp.concatenate([lag_col] * (cols // TILE), axis=1)
    pick = jnp.where(lag_col == iota((cols, cols), 1), 1.0, 0.0).astype(BF16)
    pick_t = jnp.where(lag == iota((cols, cols), 0), 1.0, 0.0).astype(BF16)
    pick_ref[...] = pick
    pick_t_ref[...] = pick_t
    zp_ref[...] = dot(pick, lagged).astype(BF16)

    for off in range(1, nz):
        when(owner(z), lambda: slice_copy(z, behind(off), off).wait_recv())
        edge_copy(z, behind(off), off).wait_recv()

    def total():
        out = part[0]
        for i in range(1, nz):
            out = out + part[i]
        mine[...] = out

    when(owner(z), total)
    all_edge[g] = cls_edge[...]

    def sum_copy(to, frm):
        return remote(mine, prior.at[frm], send2.at[to], recv2.at[frm], b, to)

    def edges_copy(to, frm):
        return remote(cls_edge, all_edge.at[frm], send2e.at[to], recv2e.at[frm], b, to)

    for h in range(1, ngrp):
        @pl.when(h > g)
        def _():
            when(owner(z), lambda: sum_copy(h, g).start())
            edges_copy(h, g).start()
    for h in range(ngrp - 1):
        @pl.when(h < g)
        def _():
            when(owner(z), lambda: sum_copy(g, h).wait_recv())

    def prefix():
        out = mine[...]
        for h in range(ngrp - 1):
            out = out + prior[h]
        whole[c, z] = out

    when(owner(z), prefix)

    def whole_copy(to, frm, off):
        return remote(whole.at[c, frm], whole.at[c, frm], send3.at[off], recv3.at[c, frm], 2 * to + c, g)

    def pair_copy(cls, frm):
        return remote(whole.at[cls, frm], whole.at[cls, frm], send3p.at[frm], recv3.at[cls, frm], partner, g)

    for off in range(1, nz):
        when(owner(z), lambda: whole_copy(ahead(off), z, off).start())
    when(owner(z), lambda: pair_copy(c, z).start())
    for h in range(ngrp - 1):
        @pl.when(h < g)
        def _():
            edges_copy(g, h).wait_recv()
    swap_edges = remote(all_edge, other_edge, send_pe, recv_pe, partner, g)
    swap_edges.start()
    ps[...] = jnp.zeros_like(ps)
    pe[...] = jnp.zeros_like(pe)
    tl[...] = jnp.zeros_like(tl)
    dm[...] = jnp.zeros_like(dm)
    miss[...] = jnp.zeros_like(miss)
    lane3 = iota((nblk, 16, TILE), 2)
    left = iota((nblk, 8, TILE), 2) < sensors
    swap_edges.wait_recv()

    def group_edges(h, carry):
        ours, theirs = all_edge[h].astype(F32), other_edge[h].astype(F32)
        first = jnp.where(c == 0, ours, theirs)
        second = jnp.where(c == 0, theirs, ours)
        e = jnp.stack([first, second], axis=1).reshape(nblk, 16, TILE)
        turned = pltpu.roll(e.reshape(nblk * 16, TILE), sensors, 1).reshape(nblk, 16, TILE)
        lo = jnp.where(lane3 < sensors, e, turned)
        hi = jnp.where(lane3 < sensors, turned, e)
        ps[0, 0:8, :] = tl[...]
        ps[1:, 0:8, :] = lo[: nblk - 1, 8:16, :]
        tl[...] = lo[nblk - 1, 8:16, :]
        pe[:, 0:8, :] = hi[:, 8:16, :]
        head = lo[:, 0:8, :].reshape(half, TILE)
        for i in range(LAGS // 2):
            even, odd = 2 * i + 1, 2 * i + 2
            for ref, at in ((ps, 0), (pe, half)):
                piece = jnp.where(left, ref[:, pl.ds(8 - even, 8), :], ref[:, pl.ds(8 - odd, 8), :])
                vt[at : at + half, i * TILE : (i + 1) * TILE] = piece.reshape(half, TILE)
        edges = vt[...].astype(BF16)
        turned_edges = dot(edges, pick_t_ref[...])
        signed = jnp.where(iota(turned_edges.shape, 0) < half, turned_edges, -turned_edges)
        dm[...] += dot(signed.T.astype(BF16), turned_edges.astype(BF16))
        miss[...] += dot(head.T.astype(BF16), edges[:half])[:sensors, :]
        return carry

    lax.fori_loop(0, g + 1, group_edges, 0)
    own = vt[pl.ds(pl.multiple_of(b * 8, 8), 8), :]
    own = jnp.concatenate([own, jnp.zeros((TILE - 8, cols), F32)], axis=0).astype(BF16)
    rim = dot(own, pick_t_ref[...]).T
    zp_ref[:, :TILE] = (zp_ref[:, :TILE].astype(F32) + rim).astype(BF16)

    for off in range(1, nz):
        frm = behind(off)

        def forward():
            whole_copy(z, frm, off).wait_recv()
            pair_copy(c, frm).start()

        when(owner(frm), forward)
    for i in range(nso):
        pair_copy(1 - c, i).wait_recv()
    for s in range(ns):
        sum_ref[s * per : (s + 1) * per, :] = whole[s % 2, s // 2]
    swap.wait_send()
    swap_edges.wait_send()
    for i in range(nso):
        pair_copy(c, i).wait_send()
    for off in range(1, nz):
        when(owner(ahead(off)), lambda: slice_copy(ahead(off), z, off).wait_send())
        edge_copy(ahead(off), z, off).wait_send()
        when(owner(z), lambda: whole_copy(ahead(off), z, off).wait_send())
    for h in range(1, ngrp):
        @pl.when(h > g)
        def _():
            when(owner(z), lambda: sum_copy(h, g).wait_send())
            edges_copy(h, g).wait_send()


def lower_inverse(block, out_ref):
    n = TILE // 8
    lane, sub = iota((8, TILE), 1), iota((8, TILE), 0)
    x = [block[8 * r : 8 * r + 8, :] for r in range(n)]

    def rep_lane(v, j):
        return jnp.broadcast_to(v[:, j : j + 1], (8, TILE))

    def rep_row(v, i):
        return jnp.broadcast_to(v[i : i + 1, :], (8, TILE))

    def inverse(p):
        return pl.reciprocal(p, approx=True)

    for q in range(n):
        first = 8 * q
        last = q == n - 1
        cols = [rep_lane(x[q], first + j) for j in range(8)]
        t = {(i, j): rep_row(cols[j], i) for j in range(8) for i in range(j, 8)}
        inside = (lane >= first) & (lane < first + 8)
        aug = jnp.where(inside, jnp.where(lane - first == sub, 1.0, 0.0), x[q])
        y = [rep_row(aug, i) for i in range(8)]
        inv, l, scaled = [None] * 8, {}, [None] * 8
        if not last:
            m = [rep_lane(x[q + 1], first + j) for j in range(8)]
            following = jnp.where(inside, 0.0, x[q + 1])
        for j in range(0, 8, 2):
            a, b, c = t[j, j], t[j + 1, j], t[j + 1, j + 1]
            det = a * c - b * b
            ia, idet = inverse(a), inverse(det)
            ic = a * idet
            inv[j], inv[j + 1] = ia, ic
            rest = range(j + 2, 8)
            for i in range(j + 1, 8):
                l[i, j] = t[i, j] * ia
            e = {i: t[i, j + 1] - l[i, j] * b for i in rest}
            for k in rest:
                for i in range(k, 8):
                    t[i, k] = (t[i, k] - l[i, j] * t[k, j]) - (e[i] * e[k]) * ic
            for i in rest:
                l[i, j + 1] = e[i] * ic
            y[j + 1] = y[j + 1] - l[j + 1, j] * y[j]
            for i in rest:
                y[i] = (y[i] - l[i, j] * y[j]) - l[i, j + 1] * y[j + 1]
            if not last:
                la = m[j] * ia
                em = m[j + 1] - la * b
                lc = em * ic
                for k in rest:
                    m[k] = (m[k] - la * t[k, j]) - lc * e[k]
                following = (following - la * y[j]) - lc * y[j + 1]
            scaled[j] = y[j] * lax.rsqrt(a)
            scaled[j + 1] = y[j + 1] * lax.rsqrt(det * ia)
        rows = scaled[0]
        for i in range(1, 8):
            rows = jnp.where(sub == i, scaled[i], rows)
        out_ref[first : first + 8, :] = jnp.where(lane < first + 8, rows, 0.0)
        if last:
            break
        x[q + 1] = following
        if q + 2 == n:
            continue
        gs = [None] * 8
        for i in range(7, -1, -1):
            acc = y[i] * inv[i]
            for k in range(7, i, -1):
                acc = acc - l[k, i] * gs[k]
            gs[i] = acc
        for r in range(q + 2, n):
            new = jnp.where(inside, 0.0, x[r])
            for j in range(7, -1, -1):
                new = new - rep_lane(x[r], first + j) * gs[j]
            x[r] = new


def fit_kernel(nblk, x_ref, pick_ref, pick_t_ref, zp_ref, dm_ref, miss_ref, c_ref, fac_ref, coef_ref, res_ref,
               a, u, li, w, v, d, row, li_now, parts, dn):
    b, g = lax.axis_index("blk"), lax.axis_index("grp")
    cols = a.shape[0]
    sensors, rows = x_ref.shape
    more = jnp.concatenate([miss_ref[...], jnp.zeros((sensors, TILE), F32)], axis=1)
    c = c_ref[...] + pltpu.roll(more, sensors, 1)
    cm = jnp.where(iota(c.shape, 1) < sensors, 0.5 * c, c)
    cr = pltpu.roll(cm, sensors, 1)
    a[...] = jnp.zeros_like(a)
    for i in range(LAGS):
        base = sensors * (i - i % 2)
        a[sensors * i : sensors * (i + 1), base:cols] = (cr if i % 2 else cm)[:, : cols - base]
    gu = a[:, :cols]
    ridge = (ridge_weight * nblk) * (g + 1).astype(F32)
    gram = gu + gu.T
    cross = jnp.concatenate([c, jnp.zeros_like(c)], axis=0).T[sensors : sensors + cols, :]
    both = jnp.concatenate([gram, cross], axis=1)
    for i, piece in enumerate(split3(both)):
        parts[i] = piece

    def assemble(r):
        pick = pick_ref[pl.ds(r, TILE), :]
        turned = dot(pick, parts[0]) + dot(pick, parts[1]) + dot(pick, parts[2])
        hi, mid, low = split3(turned[:, :cols])
        pick_t = pick_t_ref[...]
        eye = jnp.where(iota((TILE, cols), 0) + r == iota((TILE, cols), 1), ridge, 0.0)
        gram = dot(hi, pick_t) + dot(mid, pick_t) + dot(low, pick_t) + (dm_ref[pl.ds(r, TILE), :] + eye)
        a[pl.ds(r, TILE), :] = jnp.concatenate([gram, turned[:, cols:]], axis=1)

    steps = cols // TILE
    u[...] = jnp.zeros_like(u)
    li[...] = jnp.zeros_like(li)
    assemble(0)
    d[...] = a[0:TILE, 0:TILE]

    row[...] = jnp.zeros_like(row)

    def factor_rows(r):
        panel = exact_dot(li[pl.ds(r, TILE), :], row[...])
        u[pl.ds(r, TILE), :] = jnp.where(iota(panel.shape, 1) >= iota(panel.shape, 0) + r, panel, 0.0)

    def eliminate(k, carry):
        r0 = pl.multiple_of(k * TILE, TILE)
        before = pl.multiple_of(jnp.maximum(k - 1, 0) * TILE, TILE)
        r1 = pl.multiple_of(jnp.minimum(k + 1, steps - 1) * TILE, TILE)
        factor_rows(before)
        v[pl.ds(before, TILE), :] = exact_dot(li[pl.ds(before, TILE), :].T, u[pl.ds(before, TILE), :])
        row[...] = a[pl.ds(r0, TILE), :] - exact_dot(u[:, pl.ds(r0, TILE)].T, u[...])
        above = u[:, pl.ds(r1, TILE)]
        dn[...] = exact_dot(above.T, above)
        assemble(r1)
        lower_inverse(d[...], li_now)
        now = li_now[...]
        li[pl.ds(r0, TILE), :] = now
        new = exact_dot(now, row[:, pl.ds(r1, TILE)])
        d[...] = (a[pl.ds(r1, TILE), pl.ds(r1, TILE)] - dn[...]) - exact_dot(new.T, new)
        return carry

    lax.fori_loop(0, steps, eliminate, 0)
    factor_rows(cols - TILE)

    end = cols - TILE
    w[end:, :] = exact_dot(li[end:, :].T, u[end:, cols:])
    for k in range(steps - 2, -1, -1):
        at, below = slice(k * TILE, (k + 1) * TILE), (k + 1) * TILE
        w[at, :] = v[at, cols:] - exact_dot(v[at, below:cols], w[below:, :])

    share = cols // nblk
    row0 = pl.multiple_of(b * share, share)
    fac_ref[0] = u[pl.ds(row0, share), :cols] * (1.0 / math.sqrt(rows * nblk))
    coef_ref[0] = w[pl.ds(row0, share), :][:, :sensors]

    hi, mid, low = split3(w[...].T[:sensors, :])
    zp = zp_ref[...]
    res_ref[0] = x_ref[...].astype(F32) - (dot(hi, zp) + dot(mid, zp) + dot(low, zp))


def on_device(nblk, ngrp, signal, lag_table, window_end):
    _, sensors, rows = signal.shape
    cols = lag_table.shape[0]
    ns = min(nblk, sensors // 8)
    per = sensors // ns
    vmem = pl.BlockSpec(memory_space=VMEM)
    dma = pltpu.SemaphoreType.DMA
    half = nblk * 8
    nz, nso = nblk // 2, ns // 2
    share = cols // nblk
    sums, x, pick, pick_t, zp, dm, miss = pl.pallas_call(
        functools.partial(share_kernel, nblk, ngrp, ns),
        out_shape=(jax.ShapeDtypeStruct((sensors, WIDE), F32),
                   jax.ShapeDtypeStruct((sensors, rows), BF16),
                   jax.ShapeDtypeStruct((cols, cols), BF16),
                   jax.ShapeDtypeStruct((cols, cols), BF16),
                   jax.ShapeDtypeStruct((cols, rows), BF16),
                   jax.ShapeDtypeStruct((cols, cols), F32),
                   jax.ShapeDtypeStruct((sensors, cols), F32)),
        in_specs=[pl.BlockSpec(memory_space=pltpu.HBM)] * 3,
        out_specs=(vmem,) * 7,
        scratch_shapes=[
            VMEM((2, nso, per, WIDE), F32), VMEM((16, TILE), BF16),
            VMEM((nso, per, WIDE), F32), VMEM((nso, per, WIDE), F32),
            VMEM((nz, per, WIDE), F32), VMEM((nz, 16, TILE), BF16),
            VMEM((ngrp, per, WIDE), F32), VMEM((ngrp, nz, 16, TILE), BF16),
            VMEM((ngrp, nz, 16, TILE), BF16),
            VMEM((per, WIDE), F32), VMEM((2, nso, per, WIDE), F32),
            VMEM((nblk, 16, TILE), F32), VMEM((nblk, 16, TILE), F32), VMEM((8, TILE), F32),
            VMEM((2 * half, cols), F32),
            dma, dma, dma((nz,)), dma((nz,)), dma((nz,)), dma((nz,)),
            dma((ngrp,)), dma((ngrp,)), dma((ngrp,)), dma((ngrp,)),
            dma, dma, dma((nz,)), dma((nso,)), dma((2, nso)),
            pltpu.SMEM((1, 1), jnp.int32), VMEM((1, cols), jnp.int32), VMEM((1, sensors, rows), BF16), dma((3,)),
        ],
        compiler_params=pltpu.CompilerParams(
            collective_id=0, has_side_effects=True, vmem_limit_bytes=32 * 1024 * 1024),
    )(window_end, signal, lag_table.reshape(1, cols))
    return pl.pallas_call(
        functools.partial(fit_kernel, nblk),
        out_shape=(jax.ShapeDtypeStruct((1, share, cols), F32),
                   jax.ShapeDtypeStruct((1, share, sensors), F32),
                   jax.ShapeDtypeStruct((1, sensors, rows), F32)),
        in_specs=[vmem] * 7,
        out_specs=(vmem, vmem, vmem),
        scratch_shapes=[
            VMEM((cols, WIDE), F32), VMEM((cols, WIDE), F32), VMEM((cols, TILE), F32),
            VMEM((cols, TILE), F32), VMEM((cols, WIDE), F32), VMEM((TILE, TILE), F32),
            VMEM((TILE, WIDE), F32), VMEM((TILE, TILE), F32), VMEM((3, cols, WIDE), BF16), VMEM((TILE, TILE), F32),
        ],
        compiler_params=pltpu.CompilerParams(vmem_limit_bytes=40 * 1024 * 1024),
    )(x, pick, pick_t, zp, dm, miss, sums)


def solution(mesh):
    return jax.shard_map(
        functools.partial(on_device, mesh.shape["blk"], mesh.shape["grp"]),
        mesh=mesh,
        in_specs=(P("grp", None, "blk"), P(), P("grp", "blk")),
        out_specs=(P("grp", "blk", None), P("grp", "blk", None), P("grp", None, "blk")),
        check_vma=False,
    )
```

```python
import functools
import math

import jax
import jax.numpy as jnp
from jax import lax
from jax.experimental import pallas as pl
from jax.experimental.pallas import tpu as pltpu
from jax.sharding import PartitionSpec as P

ridge_weight = 4.0
LAGS = 8
TILE = 128
WIDE = 640
MESH = pl.DeviceIdType.MESH
VMEM = pltpu.VMEM
F32 = jnp.float32
BF16 = jnp.bfloat16


def iota(shape, dim):
    return lax.broadcasted_iota(jnp.int32, shape, dim)


def dot(a, b):
    return jnp.dot(a, b, preferred_element_type=F32)


def dot_nt(a, b):
    return lax.dot_general(a, b, (((1,), (1,)), ((), ())), preferred_element_type=F32)


def exact_dot(a, b):
    return jnp.dot(a, b, precision=lax.Precision.HIGHEST, preferred_element_type=F32)


def split3(x):
    hi = x.astype(BF16)
    rest = x - hi.astype(F32)
    mid = rest.astype(BF16)
    low = (rest - mid.astype(F32)).astype(BF16)
    return hi, mid, low


def delayed(x, delay):
    if delay == 0:
        return x
    return jnp.where(iota(x.shape, 1) < delay, 0.0, pltpu.roll(x, delay, 1))


def moments(x, end):
    sensors, rows = x.shape
    stack = [delayed(x, d) for d in range(LAGS + 1)] + [jnp.zeros_like(x)]
    z = jnp.concatenate(stack, axis=0).astype(BF16)
    xm = jnp.where(iota(x.shape, 1) < end, x, 0.0).astype(BF16)
    c = dot_nt(xm, z)
    row, time = iota((16, rows), 0), iota((16, rows), 1)
    head_tail = jnp.where(row < 8, row, rows - 16 + row)
    last_live = jnp.where(row < 8, -1, end - 16 + row)
    sel_a = jnp.where(time == head_tail, 1.0, 0.0).astype(BF16)
    sel_b = jnp.where(time == last_live, 1.0, 0.0).astype(BF16)
    xl = jnp.concatenate([x, jnp.zeros_like(x)], axis=0).astype(BF16)
    xr = jnp.concatenate([jnp.zeros_like(x), x], axis=0).astype(BF16)
    lagged = z[sensors : sensors * (LAGS + 1), :]
    return lagged, c, (dot_nt(sel_a, xl) + dot_nt(sel_b, xr)).astype(BF16)


def share_kernel(nblk, ngrp, ns, end_hbm, x_hbm, lag_hbm,
                 sum_ref, x_out, pick_ref, pick_t_ref, zp_ref, dm, miss,
                 c_ref, e_ref, pair, acc, part, cls_edge, prior, all_edge, other_edge, mine, whole,
                 ps, pe, tl, vt,
                 send0, recv0, send1, recv1, send1e, recv1e, send2, recv2, send2e, recv2e,
                 send_pe, recv_pe, send3, send3p, recv3, end_ref, lag_ref, x_ref, fetch):
    b, g = lax.axis_index("blk"), lax.axis_index("grp")
    nz, nso, per = nblk // 2, ns // 2, part.shape[1]
    z, c = b // 2, lax.rem(b, 2)
    partner = 2 * z + 1 - c
    cols = dm.shape[0]
    half = nblk * 8
    owner = (lambda i: True) if nso == nz else (lambda i: i < nso)

    def when(cond, fn):
        if cond is True:
            fn()
        else:
            pl.when(cond)(fn)

    def remote(src, dst, send, recv, blk, grp):
        return pltpu.make_async_remote_copy(
            src_ref=src, dst_ref=dst, send_sem=send, recv_sem=recv,
            device_id=(blk, grp), device_id_type=MESH)

    def ahead(off):
        return lax.rem(z + off, nz)

    def behind(off):
        return lax.rem(z + nz - off, nz)

    loads = [pltpu.make_async_copy(src, dst, fetch.at[i])
             for i, (src, dst) in enumerate(((x_hbm, x_ref), (end_hbm, end_ref), (lag_hbm, lag_ref)))]
    for load in loads:
        load.start()
    prior[...] = jnp.zeros_like(prior)
    all_edge[...] = jnp.zeros_like(all_edge)
    barrier = pltpu.get_barrier_semaphore()
    pl.semaphore_signal(barrier, inc=1, device_id=(partner, g), device_id_type=MESH)
    for off in range(1, nz):
        pl.semaphore_signal(barrier, inc=1, device_id=(2 * ahead(off) + c, g), device_id_type=MESH)
    for off in range(1, ngrp):
        pl.semaphore_signal(barrier, inc=1, device_id=(b, lax.rem(g + off, ngrp)), device_id_type=MESH)
    for load in loads:
        load.wait()
    x = x_ref[0].astype(F32)
    sensors = x.shape[0]
    lagged, moment, e = moments(x, end_ref[0, 0])
    for s in range(ns):
        c_ref[s % 2, s // 2] = moment[s * per : (s + 1) * per, :]
    e_ref[...] = e
    pl.semaphore_wait(barrier, nz + ngrp - 1)

    swap = remote(c_ref.at[1 - c], pair, send0, recv0, partner, g)
    swap.start()

    def edge_copy(to, frm, off):
        return remote(e_ref, cls_edge.at[frm], send1e.at[off], recv1e.at[frm], 2 * to + c, g)

    def slice_copy(to, frm, off):
        return remote(acc.at[to], part.at[frm], send1.at[off], recv1.at[frm], 2 * to + c, g)

    for off in range(1, nz):
        edge_copy(ahead(off), z, off).start()
    cls_edge[z] = e
    swap.wait_recv()
    acc[...] = c_ref[c] + pair[...]
    for off in range(1, nz):
        when(owner(ahead(off)), lambda: slice_copy(ahead(off), z, off).start())
    when(owner(z), lambda: part.__setitem__(z, acc[z]))

    x_out[...] = x_ref[0]
    lag = lag_ref[...]
    lag_col = jnp.broadcast_to(lag.astype(F32), (TILE, cols)).T.astype(jnp.int32)
    lag_col = jnp.concatenate([lag_col] * (cols // TILE), axis=1)
    pick = jnp.where(lag_col == iota((cols, cols), 1), 1.0, 0.0).astype(BF16)
    pick_t = jnp.where(lag == iota((cols, cols), 0), 1.0, 0.0).astype(BF16)
    pick_ref[...] = pick
    pick_t_ref[...] = pick_t
    zp_ref[...] = dot(pick, lagged).astype(BF16)

    for off in range(1, nz):
        when(owner(z), lambda: slice_copy(z, behind(off), off).wait_recv())
        edge_copy(z, behind(off), off).wait_recv()

    def total():
        out = part[0]
        for i in range(1, nz):
            out = out + part[i]
        mine[...] = out

    when(owner(z), total)
    all_edge[g] = cls_edge[...]

    def sum_copy(to, frm):
        return remote(mine, prior.at[frm], send2.at[to], recv2.at[frm], b, to)

    def edges_copy(to, frm):
        return remote(cls_edge, all_edge.at[frm], send2e.at[to], recv2e.at[frm], b, to)

    for h in range(1, ngrp):
        @pl.when(h > g)
        def _():
            when(owner(z), lambda: sum_copy(h, g).start())
            edges_copy(h, g).start()
    for h in range(ngrp - 1):
        @pl.when(h < g)
        def _():
            when(owner(z), lambda: sum_copy(g, h).wait_recv())

    def prefix():
        out = mine[...]
        for h in range(ngrp - 1):
            out = out + prior[h]
        whole[c, z] = out

    when(owner(z), prefix)

    def whole_copy(to, frm, off):
        return remote(whole.at[c, frm], whole.at[c, frm], send3.at[off], recv3.at[c, frm], 2 * to + c, g)

    def pair_copy(cls, frm):
        return remote(whole.at[cls, frm], whole.at[cls, frm], send3p.at[frm], recv3.at[cls, frm], partner, g)

    for off in range(1, nz):
        when(owner(z), lambda: whole_copy(ahead(off), z, off).start())
    when(owner(z), lambda: pair_copy(c, z).start())
    for h in range(ngrp - 1):
        @pl.when(h < g)
        def _():
            edges_copy(g, h).wait_recv()
    swap_edges = remote(all_edge, other_edge, send_pe, recv_pe, partner, g)
    swap_edges.start()
    ps[...] = jnp.zeros_like(ps)
    pe[...] = jnp.zeros_like(pe)
    tl[...] = jnp.zeros_like(tl)
    dm[...] = jnp.zeros_like(dm)
    miss[...] = jnp.zeros_like(miss)
    lane3 = iota((nblk, 16, TILE), 2)
    left = iota((nblk, 8, TILE), 2) < sensors
    swap_edges.wait_recv()

    def group_edges(h, carry):
        ours, theirs = all_edge[h].astype(F32), other_edge[h].astype(F32)
        first = jnp.where(c == 0, ours, theirs)
        second = jnp.where(c == 0, theirs, ours)
        e = jnp.stack([first, second], axis=1).reshape(nblk, 16, TILE)
        turned = pltpu.roll(e.reshape(nblk * 16, TILE), sensors, 1).reshape(nblk, 16, TILE)
        lo = jnp.where(lane3 < sensors, e, turned)
        hi = jnp.where(lane3 < sensors, turned, e)
        ps[0, 0:8, :] = tl[...]
        ps[1:, 0:8, :] = lo[: nblk - 1, 8:16, :]
        tl[...] = lo[nblk - 1, 8:16, :]
        pe[:, 0:8, :] = hi[:, 8:16, :]
        head = lo[:, 0:8, :].reshape(half, TILE)
        for i in range(LAGS // 2):
            even, odd = 2 * i + 1, 2 * i + 2
            for ref, at in ((ps, 0), (pe, half)):
                piece = jnp.where(left, ref[:, pl.ds(8 - even, 8), :], ref[:, pl.ds(8 - odd, 8), :])
                vt[at : at + half, i * TILE : (i + 1) * TILE] = piece.reshape(half, TILE)
        edges = vt[...].astype(BF16)
        turned_edges = dot(edges, pick_t_ref[...])
        signed = jnp.where(iota(turned_edges.shape, 0) < half, turned_edges, -turned_edges)
        dm[...] += dot(signed.T.astype(BF16), turned_edges.astype(BF16))
        miss[...] += dot(head.T.astype(BF16), edges[:half])[:sensors, :]
        return carry

    lax.fori_loop(0, g + 1, group_edges, 0)
    for off in range(1, nz):
        frm = behind(off)

        def forward():
            whole_copy(z, frm, off).wait_recv()
            pair_copy(c, frm).start()

        when(owner(frm), forward)
    own = vt[pl.ds(pl.multiple_of(b * 8, 8), 8), :]
    own = jnp.concatenate([own, jnp.zeros((TILE - 8, cols), F32)], axis=0).astype(BF16)
    rim = dot(own, pick_t_ref[...]).T
    zp_ref[:, :TILE] = (zp_ref[:, :TILE].astype(F32) + rim).astype(BF16)

    for i in range(nso):
        pair_copy(1 - c, i).wait_recv()
    for s in range(ns):
        sum_ref[s * per : (s + 1) * per, :] = whole[s % 2, s // 2]
    swap.wait_send()
    swap_edges.wait_send()
    for i in range(nso):
        pair_copy(c, i).wait_send()
    for off in range(1, nz):
        when(owner(ahead(off)), lambda: slice_copy(ahead(off), z, off).wait_send())
        edge_copy(ahead(off), z, off).wait_send()
        when(owner(z), lambda: whole_copy(ahead(off), z, off).wait_send())
    for h in range(1, ngrp):
        @pl.when(h > g)
        def _():
            when(owner(z), lambda: sum_copy(h, g).wait_send())
            edges_copy(h, g).wait_send()


def lower_inverse(block, out_ref):
    n = TILE // 8
    lane, sub = iota((8, TILE), 1), iota((8, TILE), 0)
    x = [block[8 * r : 8 * r + 8, :] for r in range(n)]

    def rep_lane(v, j):
        return jnp.broadcast_to(v[:, j : j + 1], (8, TILE))

    def rep_row(v, i):
        return jnp.broadcast_to(v[i : i + 1, :], (8, TILE))

    def inverse(p):
        return pl.reciprocal(p, approx=True)

    for q in range(n):
        first = 8 * q
        last = q == n - 1
        cols = [rep_lane(x[q], first + j) for j in range(8)]
        t = {(i, j): rep_row(cols[j], i) for j in range(8) for i in range(j, 8)}
        inside = (lane >= first) & (lane < first + 8)
        aug = jnp.where(inside, jnp.where(lane - first == sub, 1.0, 0.0), x[q])
        y = [rep_row(aug, i) for i in range(8)]
        inv, l, scaled = [None] * 8, {}, [None] * 8
        if not last:
            m = [rep_lane(x[q + 1], first + j) for j in range(8)]
            following = jnp.where(inside, 0.0, x[q + 1])
        for j in range(0, 8, 2):
            a, b, c = t[j, j], t[j + 1, j], t[j + 1, j + 1]
            det = a * c - b * b
            ia, idet = inverse(a), inverse(det)
            ic = a * idet
            inv[j], inv[j + 1] = ia, ic
            rest = range(j + 2, 8)
            for i in range(j + 1, 8):
                l[i, j] = t[i, j] * ia
            e = {i: t[i, j + 1] - l[i, j] * b for i in rest}
            for k in rest:
                for i in range(k, 8):
                    t[i, k] = (t[i, k] - l[i, j] * t[k, j]) - (e[i] * e[k]) * ic
            for i in rest:
                l[i, j + 1] = e[i] * ic
            y[j + 1] = y[j + 1] - l[j + 1, j] * y[j]
            for i in rest:
                y[i] = (y[i] - l[i, j] * y[j]) - l[i, j + 1] * y[j + 1]
            if not last:
                la = m[j] * ia
                em = m[j + 1] - la * b
                lc = em * ic
                for k in rest:
                    m[k] = (m[k] - la * t[k, j]) - lc * e[k]
                following = (following - la * y[j]) - lc * y[j + 1]
            scaled[j] = y[j] * lax.rsqrt(a)
            scaled[j + 1] = y[j + 1] * lax.rsqrt(det * ia)
        rows = scaled[0]
        for i in range(1, 8):
            rows = jnp.where(sub == i, scaled[i], rows)
        out_ref[first : first + 8, :] = jnp.where(lane < first + 8, rows, 0.0)
        if last:
            break
        x[q + 1] = following
        if q + 2 == n:
            continue
        gs = [None] * 8
        for i in range(7, -1, -1):
            acc = y[i] * inv[i]
            for k in range(7, i, -1):
                acc = acc - l[k, i] * gs[k]
            gs[i] = acc
        for r in range(q + 2, n):
            new = jnp.where(inside, 0.0, x[r])
            for j in range(7, -1, -1):
                new = new - rep_lane(x[r], first + j) * gs[j]
            x[r] = new


def fit_kernel(nblk, x_ref, pick_ref, pick_t_ref, zp_ref, dm_ref, miss_ref, c_ref, fac_ref, coef_ref, res_ref,
               a, u, li, w, v, d, row, li_now, parts, dn):
    b, g = lax.axis_index("blk"), lax.axis_index("grp")
    cols = a.shape[0]
    sensors, rows = x_ref.shape
    more = jnp.concatenate([miss_ref[...], jnp.zeros((sensors, TILE), F32)], axis=1)
    c = c_ref[...] + pltpu.roll(more, sensors, 1)
    cm = jnp.where(iota(c.shape, 1) < sensors, 0.5 * c, c)
    cr = pltpu.roll(cm, sensors, 1)
    a[...] = jnp.zeros_like(a)
    for i in range(LAGS):
        base = sensors * (i - i % 2)
        a[sensors * i : sensors * (i + 1), base:cols] = (cr if i % 2 else cm)[:, : cols - base]
    gu = a[:, :cols]
    ridge = (ridge_weight * nblk) * (g + 1).astype(F32)
    gram = gu + gu.T
    cross = jnp.concatenate([c, jnp.zeros_like(c)], axis=0).T[sensors : sensors + cols, :]
    both = jnp.concatenate([gram, cross], axis=1)
    for i, piece in enumerate(split3(both)):
        parts[i] = piece

    def assemble(r):
        pick = pick_ref[pl.ds(r, TILE), :]
        turned = dot(pick, parts[0]) + dot(pick, parts[1]) + dot(pick, parts[2])
        hi, mid, low = split3(turned[:, :cols])
        pick_t = pick_t_ref[...]
        eye = jnp.where(iota((TILE, cols), 0) + r == iota((TILE, cols), 1), ridge, 0.0)
        gram = dot(hi, pick_t) + dot(mid, pick_t) + dot(low, pick_t) + (dm_ref[pl.ds(r, TILE), :] + eye)
        a[pl.ds(r, TILE), :] = jnp.concatenate([gram, turned[:, cols:]], axis=1)

    steps = cols // TILE
    u[...] = jnp.zeros_like(u)
    li[...] = jnp.zeros_like(li)
    assemble(0)
    d[...] = a[0:TILE, 0:TILE]

    row[...] = jnp.zeros_like(row)

    def factor_rows(r):
        panel = exact_dot(li[pl.ds(r, TILE), :], row[...])
        u[pl.ds(r, TILE), :] = jnp.where(iota(panel.shape, 1) >= iota(panel.shape, 0) + r, panel, 0.0)

    def eliminate(k, carry):
        r0 = pl.multiple_of(k * TILE, TILE)
        before = pl.multiple_of(jnp.maximum(k - 1, 0) * TILE, TILE)
        r1 = pl.multiple_of(jnp.minimum(k + 1, steps - 1) * TILE, TILE)
        factor_rows(before)
        v[pl.ds(before, TILE), :] = exact_dot(li[pl.ds(before, TILE), :].T, u[pl.ds(before, TILE), :])
        row[...] = a[pl.ds(r0, TILE), :] - exact_dot(u[:, pl.ds(r0, TILE)].T, u[...])
        above = u[:, pl.ds(r1, TILE)]
        dn[...] = exact_dot(above.T, above)
        assemble(r1)
        lower_inverse(d[...], li_now)
        now = li_now[...]
        li[pl.ds(r0, TILE), :] = now
        new = exact_dot(now, row[:, pl.ds(r1, TILE)])
        d[...] = (a[pl.ds(r1, TILE), pl.ds(r1, TILE)] - dn[...]) - exact_dot(new.T, new)
        return carry

    lax.fori_loop(0, steps, eliminate, 0)
    factor_rows(cols - TILE)

    end = cols - TILE
    w[end:, :] = exact_dot(li[end:, :].T, u[end:, cols:])
    for k in range(steps - 2, -1, -1):
        at, below = slice(k * TILE, (k + 1) * TILE), (k + 1) * TILE
        w[at, :] = v[at, cols:] - exact_dot(v[at, below:cols], w[below:, :])

    share = cols // nblk
    row0 = pl.multiple_of(b * share, share)
    fac_ref[0] = u[pl.ds(row0, share), :cols] * (1.0 / math.sqrt(rows * nblk))
    coef_ref[0] = w[pl.ds(row0, share), :][:, :sensors]

    hi, mid, low = split3(w[...].T[:sensors, :])
    zp = zp_ref[...]
    res_ref[0] = x_ref[...].astype(F32) - (dot(hi, zp) + dot(mid, zp) + dot(low, zp))


def on_device(nblk, ngrp, signal, lag_table, window_end):
    _, sensors, rows = signal.shape
    cols = lag_table.shape[0]
    ns = min(nblk, sensors // 8)
    per = sensors // ns
    vmem = pl.BlockSpec(memory_space=VMEM)
    dma = pltpu.SemaphoreType.DMA
    half = nblk * 8
    nz, nso = nblk // 2, ns // 2
    share = cols // nblk
    sums, x, pick, pick_t, zp, dm, miss = pl.pallas_call(
        functools.partial(share_kernel, nblk, ngrp, ns),
        out_shape=(jax.ShapeDtypeStruct((sensors, WIDE), F32),
                   jax.ShapeDtypeStruct((sensors, rows), BF16),
                   jax.ShapeDtypeStruct((cols, cols), BF16),
                   jax.ShapeDtypeStruct((cols, cols), BF16),
                   jax.ShapeDtypeStruct((cols, rows), BF16),
                   jax.ShapeDtypeStruct((cols, cols), F32),
                   jax.ShapeDtypeStruct((sensors, cols), F32)),
        in_specs=[pl.BlockSpec(memory_space=pltpu.HBM)] * 3,
        out_specs=(vmem,) * 7,
        scratch_shapes=[
            VMEM((2, nso, per, WIDE), F32), VMEM((16, TILE), BF16),
            VMEM((nso, per, WIDE), F32), VMEM((nso, per, WIDE), F32),
            VMEM((nz, per, WIDE), F32), VMEM((nz, 16, TILE), BF16),
            VMEM((ngrp, per, WIDE), F32), VMEM((ngrp, nz, 16, TILE), BF16),
            VMEM((ngrp, nz, 16, TILE), BF16),
            VMEM((per, WIDE), F32), VMEM((2, nso, per, WIDE), F32),
            VMEM((nblk, 16, TILE), F32), VMEM((nblk, 16, TILE), F32), VMEM((8, TILE), F32),
            VMEM((2 * half, cols), F32),
            dma, dma, dma((nz,)), dma((nz,)), dma((nz,)), dma((nz,)),
            dma((ngrp,)), dma((ngrp,)), dma((ngrp,)), dma((ngrp,)),
            dma, dma, dma((nz,)), dma((nso,)), dma((2, nso)),
            pltpu.SMEM((1, 1), jnp.int32), VMEM((1, cols), jnp.int32), VMEM((1, sensors, rows), BF16), dma((3,)),
        ],
        compiler_params=pltpu.CompilerParams(
            collective_id=0, has_side_effects=True, vmem_limit_bytes=32 * 1024 * 1024),
    )(window_end, signal, lag_table.reshape(1, cols))
    return pl.pallas_call(
        functools.partial(fit_kernel, nblk),
        out_shape=(jax.ShapeDtypeStruct((1, share, cols), F32),
                   jax.ShapeDtypeStruct((1, share, sensors), F32),
                   jax.ShapeDtypeStruct((1, sensors, rows), F32)),
        in_specs=[vmem] * 7,
        out_specs=(vmem, vmem, vmem),
        scratch_shapes=[
            VMEM((cols, WIDE), F32), VMEM((cols, WIDE), F32), VMEM((cols, TILE), F32),
            VMEM((cols, TILE), F32), VMEM((cols, WIDE), F32), VMEM((TILE, TILE), F32),
            VMEM((TILE, WIDE), F32), VMEM((TILE, TILE), F32), VMEM((3, cols, WIDE), BF16), VMEM((TILE, TILE), F32),
        ],
        compiler_params=pltpu.CompilerParams(vmem_limit_bytes=40 * 1024 * 1024),
    )(x, pick, pick_t, zp, dm, miss, sums)


def solution(mesh):
    return jax.shard_map(
        functools.partial(on_device, mesh.shape["blk"], mesh.shape["grp"]),
        mesh=mesh,
        in_specs=(P("grp", None, "blk"), P(), P("grp", "blk")),
        out_specs=(P("grp", "blk", None), P("grp", "blk", None), P("grp", None, "blk")),
        check_vma=False,
    )
```
